32 devices in a mesh: dp: 16 (over z, y, core), tensor: 2 (over x).
Axes of the slice: x: 2, y: 2, z: 4, core: 2. Of those that a mesh axis runs over, the one named last changes fastest.
Arguments:
- stream: bfloat16 [32, 512, 1024], P('dp', 'tensor'), may hold values from -6 to 6
- lengths: int32 [32], replicated, may hold values from 64 to 512, as said below
- assignment: int32 [32], P('dp'), may hold values from 0 to 31, each once
- cotangent: bfloat16 [32, 512, 1024], P('dp', 'tensor'), may hold values from -6 to 6
- w_qkv: bfloat16 [1024, 3, 1024], P('dp', None, 'tensor'), may hold values from -0.1875 to 0.1875
- b_qv: bfloat16 [1024, 2], P(('tensor', 'dp')), may hold values from -3 to 3
- w_out: bfloat16 [1024, 1024], P(('tensor', 'dp')), may hold values from -1.5 to 1.5
- w_in: bfloat16 [1024, 4096], P('dp', 'tensor'), may hold values from -0.1875 to 0.1875
- b_in: bfloat16 [4096], P(('tensor', 'dp')), may hold values from -3 to 3
- w_back: bfloat16 [4096, 1024], P(('tensor', 'dp')), may hold values from -0.09375 to 0.09375
- gains: bfloat16 [1024, 2], P('dp'), may hold values from 0.099609375 to 1.8984375
- shifts: bfloat16 [1024, 4], P('dp'), may hold values from -3 to 3
Outputs:
- layer_out: bfloat16 [32, 512, 1024], P('dp', 'tensor')
- stream_grad: bfloat16 [32, 512, 1024], P('dp', 'tensor')
- grad_qkv: float32 [1024, 3, 1024], P('dp', None, 'tensor')
- grad_bqv: float32 [1024, 2], P(('tensor', 'dp'))
- grad_out: float32 [1024, 1024], P(('tensor', 'dp'))
- grad_in: float32 [1024, 4096], P('dp', 'tensor')
- grad_bin: float32 [4096], P(('tensor', 'dp'))
- grad_back: float32 [4096, 1024], P(('tensor', 'dp'))
- grad_gains: float32 [1024, 2], P('dp')
- grad_shifts: float32 [1024, 4], P('dp')
The draws below stay inside these ranges and needn't reach their ends.
Inputs may be any that keep to these rules, and one draw needn't show every extreme that they name: `lengths`: at least one sequence has exactly 512 true tokens. `assignment`: each sequence is held by exactly one slot.
All inputs are finite; a program needn't handle non-finite values.
Results may differ from the reference program's by a relative error of at most 0.02.
Values may be sent and summed in bfloat16 or wider, within the bound.
No kernel may reach another device: no remote copies, remote signals or barrier semaphores. Data moves between devices by JAX's collectives and lax.ppermute only.
A program may use at most 192 MiB of HBM per device.

```python
import math
import jax
import jax.numpy as jnp
from jax import lax

D = 1024
HD = 64
FF = 4096
LEN = 512
SEQS = 32


def draw_lengths(key, part):
    key = jax.random.fold_in(key, 7)
    first_key, second_key = jax.random.split(key)
    slots = jnp.arange(SEQS, dtype=jnp.int32)
    ceiling = LEN // 4 + 3 * LEN // 4 * slots // max(SEQS - 1, 1)
    drawn = jax.random.randint(first_key, (SEQS,), ceiling // 2, ceiling + 1)
    longest = jax.random.randint(second_key, (), 0, SEQS)
    return jnp.where(slots == longest, LEN, drawn).astype(jnp.int32)


def block_levels(rng, extent, pieces, smallest, largest):
    factor_of, own = 1.0, jax.random.fold_in(rng, 6)
    for axis_at, blocks in pieces:
        steps = jnp.exp(jax.random.uniform(jax.random.fold_in(own, axis_at), (blocks,), jnp.float32, smallest / len(pieces), largest / len(pieces)))
        factor_of = factor_of * jnp.repeat(steps, extent[axis_at] // blocks).reshape([-1 if axis == axis_at else 1 for axis in range(len(extent))])
    return factor_of


def scatter_about(stream_key, dims, deviation, limit, cuts=(), kind=jnp.bfloat16):
    entries = jax.random.normal(stream_key, dims, jnp.float32) * deviation
    if len(cuts) > 0:
        entries = block_levels(stream_key, dims, cuts, -0.22, 0.18) * entries
    return jnp.clip(entries, min=-limit, max=limit).astype(kind)


def setup_inputs(seed: int = 0) -> dict:
    arg_keys = jax.random.split(jax.random.key(seed), 13)
    stream = scatter_about(arg_keys[0], (SEQS, LEN, D), 1.0, 6.0, ((0, 16), (1, 2)))
    lengths = draw_lengths(jax.random.fold_in(arg_keys[12], 71), 0)
    assignment = jax.random.permutation(arg_keys[2], SEQS).astype(jnp.int32)
    cotangent = scatter_about(arg_keys[3], (SEQS, LEN, D), 1.0, 6.0, ((0, 16), (1, 2)))
    w_qkv = scatter_about(arg_keys[4], (D, 3, D), D ** -0.5, 0.1875, ((0, 16), (2, 2)))
    b_qv = scatter_about(arg_keys[5], (D, 2), 0.5, 3.0, ((0, 32),))
    w_out = scatter_about(arg_keys[6], (D, D), (D // 64) ** -0.5, 1.5, ((0, 32),))
    w_in = scatter_about(arg_keys[7], (D, FF), D ** -0.5, 0.1875, ((0, 16), (1, 2)))
    b_in = scatter_about(arg_keys[8], (FF,), 0.5, 3.0, ((0, 32),))
    w_back = scatter_about(arg_keys[9], (FF, D), FF ** -0.5, 0.09375, ((0, 32),))
    gains = jnp.clip(1.0 + 0.18 * jax.random.normal(arg_keys[10], (D, 2), jnp.float32), 0.099609375, 1.8984375).astype(jnp.bfloat16)
    shifts = scatter_about(arg_keys[11], (D, 4), 0.5, 3.0, ((0, 16),))
    return dict(stream=stream, lengths=lengths, assignment=assignment, cotangent=cotangent, w_qkv=w_qkv, b_qv=b_qv, w_out=w_out, w_in=w_in, b_in=b_in, w_back=w_back, gains=gains, shifts=shifts)


@jax.custom_vjp
def low(v):
    return lax.optimization_barrier(v.astype(jnp.bfloat16)).astype(jnp.float32)

@jax.custom_vjp
def low_back(v):
    return v

def low_keep(v):
    return (low(v), None)

def low_pass(kept, grad):
    return (grad,)

def back_keep(v):
    return (v, None)

def back_low(kept, grad):
    return (low(grad),)
low.defvjp(low_keep, low_pass)
low_back.defvjp(back_keep, back_low)

def norm_rows(summed, gain, offset):
    centred = summed - lax.optimization_barrier(jnp.mean(summed, axis=-1, keepdims=True))
    variance = lax.optimization_barrier(jnp.mean(centred * centred, axis=-1, keepdims=True))
    return centred * lax.rsqrt(variance + 1e-06) * gain + offset

def exact_gelu(values):
    return jax.nn.gelu(values, approximate=False)

def layer(stream, seq_lengths, w_qkv, b_qv, w_out, w_in, b_in, w_back, gains, shifts):
    highest = lax.Precision.HIGHEST
    group, length, width = stream.shape
    shape_heads = (group, length, width // HD, HD)
    projected_rows = jnp.einsum('gld,dcf->glcf', stream, w_qkv, precision=highest)
    queries = low_back(low(projected_rows[:, :, 0] + b_qv[:, 0])).reshape(shape_heads)
    key_rows = low_back(low(projected_rows[:, :, 1])).reshape(shape_heads)
    value_rows = low_back(low(projected_rows[:, :, 2] + b_qv[:, 1])).reshape(shape_heads)
    products = low_back(jnp.einsum('gqhe,gkhe->ghqk', queries, key_rows, precision=highest))
    allowed = jnp.arange(length, dtype=jnp.int32)[None, :] < seq_lengths[:, None]
    scores = jnp.where(allowed[:, None, None, :], products * HD ** (-0.5), -1e+30)
    highest_score = lax.optimization_barrier(jnp.max(scores, axis=-1, keepdims=True))
    expo = jnp.exp(scores - highest_score)
    weights = expo / lax.optimization_barrier(jnp.sum(expo, axis=-1, keepdims=True))
    context_rows = jnp.einsum('ghqk,gkhe->gqhe', low(weights), value_rows, precision=highest)
    context_rows = low_back(low(context_rows.reshape(group, length, width)))
    attended = low_back(jnp.einsum('glf,fd->gld', context_rows, w_out, precision=highest) + shifts[:, 1])
    mixed = norm_rows(stream + attended, gains[:, 0], shifts[:, 0])
    inner = low_back(jnp.einsum('gld,df->glf', low(mixed), w_in, precision=highest) + b_in)
    hidden = low(exact_gelu(inner))
    branch = low_back(jnp.einsum('glf,fd->gld', hidden, w_back, precision=highest) + shifts[:, 3])
    return norm_rows(mixed + branch, gains[:, 1], shifts[:, 2])

def reference(stream, lengths, assignment, cotangent, w_qkv, b_qv, w_out, w_in, b_in, w_back, gains, shifts):
    params = tuple((operand.astype(jnp.float32) for operand in (w_qkv, b_qv, w_out, w_in, b_in, w_back, gains, shifts)))
    count = jnp.sum(lengths).astype(jnp.float32)
    factor = SEQS * LEN / count
    slot_len = lengths[assignment.astype(jnp.int32)].astype(jnp.int32)
    group = math.gcd(SEQS, max(1, 4096 // LEN))
    blocks = SEQS // group
    stream_blocks = stream.reshape(blocks, group, LEN, D)
    length_blocks = slot_len.reshape(blocks, group)
    cot_blocks = cotangent.reshape(blocks, group, LEN, D)

    def one_block(totals, item):
        block_stream, block_lengths, block_cot = item
        live = (jnp.arange(LEN, dtype=jnp.int32)[None, :] < block_lengths[:, None]).astype(jnp.float32)
        seed_grad = block_cot.astype(jnp.float32) * live[:, :, None] * factor

        def forward(inputs, *weights_all):
            return layer(inputs, block_lengths, *weights_all)
        result, pull = jax.vjp(forward, block_stream.astype(jnp.float32), *params)
        grads = pull(seed_grad)
        totals = jax.tree.map(jnp.add, totals, tuple(grads[1:]))
        return (totals, (result.astype(jnp.bfloat16), grads[0].astype(jnp.bfloat16)))
    zeros = tuple((jnp.zeros_like(operand) for operand in params))
    totals, (outputs, stream_grads) = lax.scan(one_block, zeros, (stream_blocks, length_blocks, cot_blocks))
    layer_out = outputs.reshape(SEQS, LEN, D)
    stream_grad = stream_grads.reshape(SEQS, LEN, D)
    return (layer_out, stream_grad, totals[0], totals[1], totals[2], totals[3], totals[4], totals[5], totals[6], totals[7])
```

```python
import functools

import jax
import jax.numpy as jnp
from jax import lax
from jax.experimental import pallas as pl
from jax.experimental.pallas import tpu as pltpu
from jax.sharding import PartitionSpec as P

HD = 64
BF = jnp.bfloat16
F32 = jnp.float32
VMEM = 56 * 1024 * 1024


def norm_rows(summed, gain, offset):
    centred = summed - jnp.mean(summed, axis=-1, keepdims=True)
    variance = jnp.mean(centred * centred, axis=-1, keepdims=True)
    return centred * lax.rsqrt(variance + 1e-06) * gain + offset


def exact_gelu(values):
    return jax.nn.gelu(values, approximate=False)


def per_device(
    stream, lengths, assignment, cotangent, w_qkv, b_qv, w_out, w_in, b_in, w_back, gains, shifts
):
    count = jnp.sum(lengths).astype(jnp.float32)
    all_seqs = lengths.shape[0]
    matches = assignment[:, None] == jnp.arange(all_seqs, dtype=jnp.int32)[None, :]
    slot_len = jnp.sum(jnp.where(matches, lengths[None, :], 0), axis=1)
    (
        projection_weight,
        mixing_weight,
        up_weight,
        down_weight,
        bias_qv,
        bias_up,
        gain_all,
        shift_all,
    ) = (
        lax.all_gather(w_qkv, "dp", axis=0, tiled=True),
        lax.all_gather(w_out, "dp", axis=0, tiled=True),
        lax.all_gather(w_in, "dp", axis=0, tiled=True),
        lax.all_gather(w_back, "dp", axis=0, tiled=True),
        lax.all_gather(b_qv, "dp", axis=0, tiled=True),
        lax.all_gather(b_in, "dp", axis=0, tiled=True),
        lax.all_gather(gains, "dp", axis=0, tiled=True),
        lax.all_gather(shifts, "dp", axis=0, tiled=True),
    )
    seqs_dev, rows_dev, width = stream.shape
    full_rows = rows_dev * lax.axis_size("tensor")
    local_width = projection_weight.shape[2]
    shape_heads = (seqs_dev, full_rows, local_width // HD, HD)
    scale = HD ** (-0.5)
    gain_f = gain_all.astype(jnp.float32)
    shift_f = shift_all.astype(jnp.float32)
    bias_f = bias_qv.astype(jnp.float32)
    gathered_rows = lax.all_gather(stream, "tensor", axis=1, tiled=True)
    projected_rows = jnp.einsum(
        "bpo,orn->bprn", gathered_rows, projection_weight, preferred_element_type=jnp.float32
    )
    queries = (projected_rows[:, :, 0] + bias_f[:, 0]).astype(jnp.bfloat16).reshape(shape_heads)
    key_rows = projected_rows[:, :, 1].astype(jnp.bfloat16).reshape(shape_heads)
    value_rows = (projected_rows[:, :, 2] + bias_f[:, 1]).astype(jnp.bfloat16).reshape(shape_heads)
    allowed = jnp.arange(full_rows, dtype=jnp.int32)[None, :] < slot_len[:, None]
    products = jnp.einsum("sqhe,skhe->shqk", queries, key_rows, preferred_element_type=jnp.float32)
    scores = jnp.where(allowed[:, None, None, :], products * scale, -1e30)
    highest_score = jnp.max(scores, axis=-1, keepdims=True)
    expo = jnp.exp(scores - highest_score)
    weights = expo / jnp.sum(expo, axis=-1, keepdims=True)
    weights_low = weights.astype(jnp.bfloat16)
    context_rows = jnp.einsum(
        "shqk,skhe->sqhe", weights_low, value_rows, preferred_element_type=jnp.float32
    )
    context_rows = context_rows.reshape(seqs_dev, full_rows, local_width).astype(jnp.bfloat16)
    attention_terms = jnp.einsum(
        "kqz,zw->kqw", context_rows, mixing_weight, preferred_element_type=jnp.float32
    )
    attended = (
        lax.psum_scatter(
            attention_terms.astype(jnp.bfloat16), "tensor", scatter_dimension=1, tiled=True
        ).astype(jnp.float32)
        + shift_f[:, 1]
    )
    mixed, first_pull = jax.vjp(
        norm_rows, stream.astype(jnp.float32) + attended, gain_f[:, 0], shift_f[:, 0]
    )
    mixed_every_row = lax.all_gather(mixed.astype(jnp.bfloat16), "tensor", axis=1, tiled=True)
    inner = jnp.einsum(
        "vrw,wy->vry", mixed_every_row, up_weight, preferred_element_type=jnp.float32
    ) + bias_up.astype(jnp.float32)
    hidden, gelu_pull = jax.vjp(exact_gelu, inner)
    hidden_reduced = hidden.astype(jnp.bfloat16)
    perceptron_terms = jnp.einsum(
        "kqz,zw->kqw", hidden_reduced, down_weight, preferred_element_type=jnp.float32
    )
    branch = (
        lax.psum_scatter(
            perceptron_terms.astype(jnp.bfloat16), "tensor", scatter_dimension=1, tiled=True
        ).astype(jnp.float32)
        + shift_f[:, 3]
    )
    result, second_pull = jax.vjp(norm_rows, mixed + branch, gain_f[:, 1], shift_f[:, 2])
    position = lax.axis_index("tensor") * rows_dev + jnp.arange(rows_dev, dtype=jnp.int32)
    live = (position[None, :] < slot_len[:, None]).astype(jnp.float32)
    factor = jnp.float32(seqs_dev * lax.axis_size("dp") * full_rows) / count
    seed_grad = cotangent.astype(jnp.float32) * live[:, :, None] * factor
    grad_sum2, grad_gain2, grad_shift2 = second_pull(seed_grad)
    grad_branch = grad_sum2.astype(jnp.bfloat16)
    branch_bias_grad = jnp.sum(grad_branch.astype(jnp.float32), axis=(0, 1))
    branch_every_row = lax.all_gather(grad_branch, "tensor", axis=1, tiled=True)
    down_part = jnp.einsum(
        "irk,irt->kt", hidden_reduced, branch_every_row, preferred_element_type=jnp.float32
    )
    hidden_gradient = jnp.einsum(
        "atj,gj->atg", branch_every_row, down_weight, preferred_element_type=jnp.float32
    )
    inner_gradient = gelu_pull(hidden_gradient)[0].astype(jnp.bfloat16)
    up_bias_part = jnp.sum(inner_gradient.astype(jnp.float32), axis=(0, 1))
    up_portion = jnp.einsum(
        "pna,pnb->ab", mixed_every_row, inner_gradient, preferred_element_type=jnp.float32
    )
    mixed_partial_terms = jnp.einsum(
        "yjc,oc->yjo", inner_gradient, up_weight, preferred_element_type=jnp.float32
    )
    grad_mixed = grad_sum2 + lax.psum_scatter(
        mixed_partial_terms.astype(jnp.bfloat16), "tensor", scatter_dimension=1, tiled=True
    ).astype(jnp.float32)
    grad_sum1, grad_gain1, grad_shift1 = first_pull(grad_mixed)
    grad_attended = grad_sum1.astype(jnp.bfloat16)
    mix_bias_grad = jnp.sum(grad_attended.astype(jnp.float32), axis=(0, 1))
    attended_every_row = lax.all_gather(grad_attended, "tensor", axis=1, tiled=True)
    mixing_portion = jnp.einsum(
        "irk,irt->kt", context_rows, attended_every_row, preferred_element_type=jnp.float32
    )
    grad_context = jnp.einsum(
        "atj,gj->atg", attended_every_row, mixing_weight, preferred_element_type=jnp.float32
    )
    grad_context = grad_context.astype(jnp.bfloat16).reshape(shape_heads)
    grad_values = jnp.einsum(
        "shqk,sqhe->skhe", weights_low, grad_context, preferred_element_type=jnp.float32
    ).astype(jnp.bfloat16)
    grad_weights = jnp.einsum(
        "sqhe,skhe->shqk", grad_context, value_rows, preferred_element_type=jnp.float32
    )
    grad_scores = weights * (grad_weights - jnp.sum(weights * grad_weights, axis=-1, keepdims=True))
    grad_products = (grad_scores * scale).astype(jnp.bfloat16)
    grad_queries = jnp.einsum(
        "shqk,skhe->sqhe", grad_products, key_rows, preferred_element_type=jnp.float32
    ).astype(jnp.bfloat16)
    grad_keys = jnp.einsum(
        "shqk,sqhe->skhe", grad_products, queries, preferred_element_type=jnp.float32
    ).astype(jnp.bfloat16)
    flat_shape = (seqs_dev, full_rows, local_width)
    projection_gradient = jnp.stack(
        [
            grad_queries.reshape(flat_shape),
            grad_keys.reshape(flat_shape),
            grad_values.reshape(flat_shape),
        ],
        axis=2,
    )
    proj_bias_part = jnp.stack(
        [
            jnp.sum(grad_queries.astype(jnp.float32).reshape(flat_shape), axis=(0, 1)),
            jnp.sum(grad_values.astype(jnp.float32).reshape(flat_shape), axis=(0, 1)),
        ],
        axis=1,
    )
    projection_portion = jnp.einsum(
        "tqj,tquk->juk", gathered_rows, projection_gradient, preferred_element_type=jnp.float32
    )
    stream_terms = jnp.einsum(
        "wvjo,xjo->wvx", projection_gradient, projection_weight, preferred_element_type=jnp.float32
    )
    grad_stream = grad_sum1 + lax.psum_scatter(
        stream_terms.astype(jnp.bfloat16), "tensor", scatter_dimension=1, tiled=True
    ).astype(jnp.float32)
    gain_part = jnp.stack([grad_gain1, grad_gain2], axis=1)
    shift_part = jnp.stack([grad_shift1, mix_bias_grad, grad_shift2, branch_bias_grad], axis=1)
    proj_done, proj_bias_done, mix_done, up_done, up_bias_done, down_done, gain_done, shift_done = (
        lax.psum_scatter(
            projection_portion.astype(jnp.bfloat16), "dp", scatter_dimension=0, tiled=True
        ).astype(jnp.float32),
        lax.psum_scatter(
            proj_bias_part.astype(jnp.bfloat16), "dp", scatter_dimension=0, tiled=True
        ).astype(jnp.float32),
        lax.psum_scatter(
            mixing_portion.astype(jnp.bfloat16), "dp", scatter_dimension=0, tiled=True
        ).astype(jnp.float32),
        lax.psum_scatter(
            up_portion.astype(jnp.bfloat16), "dp", scatter_dimension=0, tiled=True
        ).astype(jnp.float32),
        lax.psum_scatter(
            up_bias_part.astype(jnp.bfloat16), "dp", scatter_dimension=0, tiled=True
        ).astype(jnp.float32),
        lax.psum_scatter(
            down_part.astype(jnp.bfloat16), "dp", scatter_dimension=0, tiled=True
        ).astype(jnp.float32),
        lax.psum_scatter(
            gain_part.astype(jnp.bfloat16), "dp", scatter_dimension=0, tiled=True
        ).astype(jnp.float32),
        lax.psum_scatter(
            shift_part.astype(jnp.bfloat16), "dp", scatter_dimension=0, tiled=True
        ).astype(jnp.float32),
    )
    gain_total, shift_total = lax.psum((gain_done, shift_done), "tensor")
    return (
        result.astype(jnp.bfloat16),
        grad_stream.astype(jnp.bfloat16),
        proj_done,
        proj_bias_done,
        mix_done,
        up_done,
        up_bias_done,
        down_done,
        gain_total,
        shift_total,
    )


def kernel(body, name, grid, in_specs, out_specs, out_shape, args, *, scratch=(), prefetch=0, deps=()):
    inputs = prefetch + len(in_specs)

    def without_deps(*refs):
        body(*refs[:inputs], *refs[inputs + len(deps) :])

    return pl.pallas_call(
        without_deps,
        grid_spec=pltpu.PrefetchScalarGridSpec(
            num_scalar_prefetch=prefetch,
            grid=grid,
            in_specs=list(in_specs) + [pl.BlockSpec(memory_space=pl.ANY)] * len(deps),
            out_specs=out_specs,
            scratch_shapes=scratch,
        ),
        out_shape=out_shape,
        compiler_params=pltpu.CompilerParams(vmem_limit_bytes=VMEM),
        name=name,
    )(*args, *deps)


def gelu_terms(v):
    density = jnp.exp(v * v * -0.5)
    t = 1.0 / (1.0 + (0.3275911 * 0.7071067811865476) * jnp.abs(v))
    poly = t * (
        0.254829592
        + t * (-0.284496736 + t * (1.421413741 + t * (-1.453152027 + t * 1.061405429)))
    )
    tail = 0.5 * poly * density
    return jnp.where(v >= 0, 1.0 - tail, tail), density * 0.3989422804014327


def dot(a, b, dims=((1,), (0,))):
    return lax.dot_general(a, b, (dims, ((), ())), preferred_element_type=F32)


def project_body(a_ref, w00, w10, w01, w11, b_ref, o_ref, *, half):
    j = pl.program_id(0)
    k = w00.shape[0]

    def go(w0, w1):
        acc = dot(a_ref[:, :k], w0[...]) + dot(a_ref[:, k:], w1[...]) + b_ref[...]
        o_ref[...] = acc.astype(o_ref.dtype)

    @pl.when(j < half)
    def _():
        go(w00, w10)

    @pl.when(j >= half)
    def _():
        go(w01, w11)


def split_specs(rows, block, half):
    low = pl.BlockSpec((rows, block), lambda j, *_: (0, jnp.minimum(j, half - 1)))
    high = pl.BlockSpec((rows, block), lambda j, *_: (0, jnp.maximum(j - half, 0)))
    return [low, low, high, high]


def project(a, w, bias, block, deps=()):
    rows, width = a.shape
    cols = w[0][0].shape[1]
    half = cols // block
    return kernel(
        functools.partial(project_body, half=half),
        "project",
        (2 * half,),
        [pl.BlockSpec((rows, width), lambda j: (0, 0))]
        + split_specs(width // 2, block, half)
        + [pl.BlockSpec((1, block), lambda j: (0, j))],
        pl.BlockSpec((rows, block), lambda j: (0, j)),
        jax.ShapeDtypeStruct((rows, 2 * cols), BF),
        (a, w[0][0], w[1][0], w[0][1], w[1][1], bias,),
        deps=deps,
    )


def up_body(place, a_ref, w00, w10, w01, w11, b_ref, h_ref, g_ref, acc, *, half):
    j = pl.program_id(0)
    k = w00.shape[0]

    def go(w0, w1):
        new = dot(a_ref[:, :k], w0[...]) + dot(a_ref[:, k:], w1[...])
        v = acc[...]
        cdf, density = gelu_terms(v)
        h_ref[...] = (v * cdf).astype(BF)
        g_ref[...] = (cdf + v * density).astype(BF)
        acc[...] = new + b_ref[...]

    @pl.when(j < half)
    def _():
        go(w00, w10)

    @pl.when(j >= half)
    def _():
        go(w01, w11)


def up_gelu(a, w, bias, place, block, deps=()):
    rows, width = a.shape
    cols = w[0][0].shape[1]
    half = cols // block
    end = 2 * half - 1
    out = jax.ShapeDtypeStruct((rows, 2 * cols), BF)

    def where(j, place):
        j = jnp.maximum(j - 1, 0)
        return (0, (j + place[0] * half) % (2 * half))

    spot = pl.BlockSpec((rows, block), where)
    low = pl.BlockSpec((width // 2, block), lambda j, place: (0, jnp.minimum(j, half - 1)))
    high = pl.BlockSpec((width // 2, block), lambda j, place: (0, jnp.clip(j - half, 0, half - 1)))
    return kernel(
        functools.partial(up_body, half=half),
        "up_gelu",
        (2 * half + 1,),
        [pl.BlockSpec((rows, width), lambda j, place: (0, 0))]
            + [low, low, high, high]
            + [pl.BlockSpec((1, block), lambda j, place: (0, jnp.minimum(j, end)))],
        [spot, spot],
        [out, out],
        (place, a, w[0][0], w[1][0], w[0][1], w[1][1], bias,),
        scratch=[pltpu.VMEM((rows, block), F32)],
        prefetch=1,
        deps=deps,
    )


def down_grad_body(place, a_ref, w_ref, g_ref, d_ref, s_ref):
    d = dot(a_ref[...], w_ref[...], ((1,), (1,)))
    d = (d * g_ref[...].astype(F32)).astype(BF)
    d_ref[...] = d
    s_ref[...] = jnp.sum(d.astype(F32), axis=0, keepdims=True)


def down_grad(a, w, g, place, block, part, deps=()):
    rows, width = a.shape
    cols = g.shape[1] // 2
    steps = cols // block

    def at(j, place):
        return (j + (place[0] ^ part) * steps)

    return kernel(
        down_grad_body,
        "down_grad",
        (steps,),
        [
                pl.BlockSpec((rows, width), lambda j, place: (0, 0)),
                pl.BlockSpec((block, width), lambda j, place: (at(j, place), 0)),
                pl.BlockSpec((rows, block), lambda j, place: (0, at(j, place))),
            ],
        [
                pl.BlockSpec((rows, block), lambda j, place: (0, j)),
                pl.BlockSpec((1, block), lambda j, place: (0, j)),
            ],
        [
            jax.ShapeDtypeStruct((rows, cols), BF),
            jax.ShapeDtypeStruct((1, cols), F32),
        ],
        (place, a, w, g,),
        prefetch=1,
        deps=deps,
    )


def head_weights(info, q, k, rows):
    own = rows // 2
    at = lax.broadcasted_iota(jnp.int32, (1, rows), 1)
    first = info[1] * own
    pos = jnp.where(at < own, at + first, at - first)
    s = dot(q, k, ((1,), (1,)))
    s = jnp.where(pos < info[0], s * HD ** (-0.5), -1e30)
    e = jnp.exp(s - jnp.max(s, axis=1, keepdims=True))
    return e * (1.0 / jnp.sum(e, axis=1, keepdims=True))


def attend_body(info, p_ref, c_ref):
    rows, lanes = c_ref.shape
    for h in range(lanes // HD):
        part = [p_ref[:, j * lanes + h * HD : j * lanes + (h + 1) * HD] for j in range(3)]
        w = head_weights(info, part[0], part[1], rows).astype(BF)
        c_ref[:, h * HD : (h + 1) * HD] = dot(w, part[2]).astype(BF)


def attend_grad_body(info, p_ref, t_ref, d_ref, s_ref):
    rows, lanes = t_ref.shape
    tn = ((0,), (0,))
    for h in range(lanes // HD):
        q, k, v = [p_ref[:, j * lanes + h * HD : j * lanes + (h + 1) * HD] for j in range(3)]
        t = t_ref[:, h * HD : (h + 1) * HD]
        w = head_weights(info, q, k, rows)
        dw = dot(t, v, ((1,), (1,)))
        ds = w * (dw - jnp.sum(w * dw, axis=1, keepdims=True)) * HD ** (-0.5)
        ds = ds.astype(BF)
        outs = (dot(ds, k), dot(ds, q, tn), dot(w.astype(BF), t, tn))
        for j in range(3):
            at = slice(j * lanes + h * HD, j * lanes + (h + 1) * HD)
            low = outs[j].astype(BF)
            d_ref[:, at] = low
            s_ref[:, at] = jnp.sum(low.astype(F32), axis=0, keepdims=True)


def attend(info, proj, lanes, part, deps=()):
    rows, cols = proj.shape
    steps = cols // (6 * lanes)
    return kernel(
        attend_body,
        "attend",
        (steps,),
        [pl.BlockSpec((rows, 3 * lanes), lambda j, info: (0, j + part * steps))],
        pl.BlockSpec((rows, lanes), lambda j, info: (0, j)),
        jax.ShapeDtypeStruct((rows, cols // 6), BF),
        (info, proj,),
        prefetch=1,
        deps=deps,
    )


def attend_grad(info, proj, top, lanes, part, deps=()):
    rows, cols = proj.shape
    steps = cols // (6 * lanes)
    return kernel(
        attend_grad_body,
        "attend_grad",
        (steps,),
        [
                pl.BlockSpec((rows, 3 * lanes), lambda j, info: (0, j + part * steps)),
                pl.BlockSpec((rows, lanes), lambda j, info: (0, j + part * steps)),
            ],
        [
                pl.BlockSpec((rows, 3 * lanes), lambda j, info: (0, j)),
                pl.BlockSpec((1, 3 * lanes), lambda j, info: (0, j)),
            ],
        [
            jax.ShapeDtypeStruct((rows, cols // 2), BF),
            jax.ShapeDtypeStruct((1, cols // 2), F32),
        ],
        (info, proj, top,),
        prefetch=1,
        deps=deps,
    )


def whole_of(v):
    return pl.BlockSpec(v.shape, lambda *_: (0,) * v.ndim)


def tile_of(v, tile):
    return pl.BlockSpec((tile, v.shape[1]), lambda j: (j, 0))


def norm_of(z):
    centred = z - jnp.mean(z, axis=1, keepdims=True)
    r = lax.rsqrt(jnp.mean(centred * centred, axis=1, keepdims=True) + 1e-06)
    return centred * r, r


def norm_grad(t, zhat, r, gain):
    gt = t * gain
    mean = jnp.mean(gt, axis=1, keepdims=True)
    return r * (gt - mean - zhat * jnp.mean(gt * zhat, axis=1, keepdims=True))


def gather_sums(s_ref, *values):
    sums = [jnp.sum(v, axis=0, keepdims=True) for v in values]
    sums += [jnp.zeros_like(sums[0])] * (8 - len(sums))
    sums = jnp.concatenate(sums, axis=0)

    @pl.when(pl.program_id(0) == 0)
    def _():
        s_ref[...] = sums

    @pl.when(pl.program_id(0) != 0)
    def _():
        s_ref[...] += sums


def mix_body(c0, c1, s_ref, w0, w1, pc, pi, v_ref, zh_ref, r_ref, m_ref, mr_ref, x_ref):
    h = w0.shape[0]
    ctx = dot(c0[...], pc[:h, :]) + dot(c1[...], pc[h:, :])
    ctx = ctx.astype(BF)
    x_ref[...] = ctx
    att = dot(ctx[:, :h], w0[...]) + dot(ctx[:, h:], w1[...]) + v_ref[3:4, :]
    zhat, r = norm_of(s_ref[...].astype(F32) + att)
    zh_ref[...] = zhat
    r_ref[...] = jnp.broadcast_to(r, r_ref.shape)
    mixed = zhat * v_ref[0:1, :] + v_ref[2:3, :]
    m_ref[...] = mixed
    mr_ref[...] = dot(mixed.astype(BF), pi[...]).astype(BF)


def mix(c0, c1, stream, w0, w1, perm_ctx, perm_in, vecs, tile, deps=()):
    rows, width = stream.shape
    full = jax.ShapeDtypeStruct((rows, width), F32)
    low = jax.ShapeDtypeStruct((rows, width), BF)
    outs = [full, jax.ShapeDtypeStruct((rows, 128), F32), full, low, low]
    return kernel(
        mix_body,
        "mix",
        (rows // tile,),
        [tile_of(v, tile) for v in (c0, c1, stream)]
        + [whole_of(v) for v in (w0, w1, perm_ctx, perm_in, vecs)],
        [tile_of(v, tile) for v in outs],
        outs,
        (c0, c1, stream, w0, w1, perm_ctx, perm_in, vecs,),
        deps=deps,
    )


def turn_body(h_ref, w_ref, m_ref, c_ref, l_ref, v_ref, o_ref, g_ref, gb_ref, s_ref):
    branch = dot(h_ref[...], w_ref[...]) + v_ref[5:6, :]
    zhat, r = norm_of(m_ref[...] + branch)
    gain = v_ref[1:2, :]
    o_ref[...] = (zhat * gain + v_ref[4:5, :]).astype(BF)
    seed = c_ref[...].astype(F32) * l_ref[:, 0:1]
    g = norm_grad(seed, zhat, r, gain)
    g_ref[...] = g
    low = g.astype(BF)
    gb_ref[...] = low
    gather_sums(s_ref, seed * zhat, seed, low.astype(F32))


def turn(h, w, mixed, cot, live, vecs, tile, deps=()):
    rows, width = mixed.shape
    full = jax.ShapeDtypeStruct((rows, width), F32)
    low = jax.ShapeDtypeStruct((rows, width), BF)
    sums = jax.ShapeDtypeStruct((8, width), F32)
    return kernel(
        turn_body,
        "turn",
        (rows // tile,),
        [tile_of(h, tile), whole_of(w)]
        + [tile_of(v, tile) for v in (mixed, cot, live)]
        + [whole_of(vecs)],
        [tile_of(v, tile) for v in (low, full, low)] + [whole_of(sums)],
        [low, full, low, sums],
        (h, w, mixed, cot, live, vecs,),
        deps=deps,
    )


def unmix_body(
    d0, d1, w00, w10, w01, w11, pi, g2, zh, r_ref, wo0, wo1, pc, v_ref, g1_ref, ga_ref, gc_ref, s_ref
):
    nt = ((1,), (1,))
    parts = [
        dot(d0[...], u[...], nt) + dot(d1[...], v[...], nt) for u, v in ((w00, w01), (w10, w11))
    ]
    back = jnp.concatenate(parts, axis=1).astype(BF)
    grad = g2[...] + dot(back, pi[...], nt)
    zhat = zh[...]
    g1 = norm_grad(grad, zhat, r_ref[:, 0:1], v_ref[0:1, :])
    g1_ref[...] = g1
    low = g1.astype(BF)
    ga_ref[...] = low
    ctx = jnp.concatenate([dot(low, wo0[...], nt), dot(low, wo1[...], nt)], axis=1)
    gc_ref[...] = dot(ctx.astype(BF), pc[...], nt).astype(BF)
    gather_sums(s_ref, grad * zhat, grad, low.astype(F32))


def unmix(d0, d1, w, perm_in, g2, zhat, r, wo0, wo1, perm_ctx, vecs, tile, deps=()):
    rows, width = g2.shape
    full = jax.ShapeDtypeStruct((rows, width), F32)
    low = jax.ShapeDtypeStruct((rows, width), BF)
    sums = jax.ShapeDtypeStruct((8, width), F32)
    ws = (w[0][0], w[1][0], w[0][1], w[1][1])
    return kernel(
        unmix_body,
        "unmix",
        (rows // tile,),
        [tile_of(d0, tile), tile_of(d1, tile)]
        + [whole_of(v) for v in ws + (perm_in,)]
        + [tile_of(v, tile) for v in (g2, zhat, r)]
        + [whole_of(v) for v in (wo0, wo1, perm_ctx, vecs)],
        [tile_of(v, tile) for v in (full, low, low)] + [whole_of(sums)],
        [full, low, low, sums],
        (d0, d1, *ws, perm_in, g2, zhat, r, wo0, wo1, perm_ctx, vecs,),
        deps=deps,
    )


def stream_body(d0, d1, w00, w10, w01, w11, pi, g1, o_ref):
    nt = ((1,), (1,))
    parts = [
        dot(d0[...], u[...], nt) + dot(d1[...], v[...], nt) for u, v in ((w00, w01), (w10, w11))
    ]
    back = jnp.concatenate(parts, axis=1).astype(BF)
    o_ref[...] = (g1[...] + dot(back, pi[...], nt)).astype(BF)


def stream_grad(d0, d1, w, perm_in, g1, tile, deps=()):
    out = jax.ShapeDtypeStruct(g1.shape, BF)
    ws = (w[0][0], w[1][0], w[0][1], w[1][1])
    return kernel(
        stream_body,
        "stream_grad",
        (g1.shape[0] // tile,),
        [tile_of(d0, tile), tile_of(d1, tile)]
        + [whole_of(v) for v in ws + (perm_in,)]
        + [tile_of(g1, tile)],
        tile_of(out, tile),
        out,
        (d0, d1, *ws, perm_in, g1,),
        deps=deps,
    )


TN = ((0,), (0,))


def rows_body(l_ref, r_ref, *refs, added, per):
    grad = dot(l_ref[...], r_ref[...], TN)
    if not added:
        refs[0][...] = grad.astype(BF)
        return
    grad = (grad + refs[0][...].astype(F32)).astype(BF)
    j = pl.program_id(0)
    for i in range(4):

        @pl.when(j // per == i)
        def _():
            refs[1 + i][...] = grad


def weight_rows(left, right, got=None, deps=()):
    tokens, k = left.shape
    n = right.shape[1]
    per = 2 if k // 8 % 128 == 0 else 1
    block = k // (4 * per)
    row = pl.BlockSpec((block, n), lambda j: (j, 0))
    outs, out_specs, more = [jax.ShapeDtypeStruct((k, n), BF)], [row], []
    if got is not None:
        outs = [jax.ShapeDtypeStruct((k // 4, n), BF)] * 4
        out_specs = [
            pl.BlockSpec((block, n), lambda j, i=i: (jnp.clip(j - per * i, 0, per - 1), 0))
            for i in range(4)
        ]
        more = [got]
    return kernel(
        functools.partial(rows_body, added=got is not None, per=per),
        "weight_rows",
        (4 * per,),
        [pl.BlockSpec((tokens, block), lambda j: (0, j)), whole_of(right)]
        + [row] * len(more),
        out_specs,
        outs,
        (left, right, *more,),
        deps=deps,
    )


def cols_body(l_ref, r0, r1, *refs, half, added):
    j = pl.program_id(0)
    turned = refs[-1]

    @pl.when(j == 0)
    def _():
        turned[...] = l_ref[...].T

    def go(r, high):
        grad = dot(turned[...], r[...])
        if not added:
            refs[0][...] = grad.astype(BF)
            return
        got, keep_a, send_a, keep_b, send_b = refs[:5]
        q = grad.shape[0] // 4
        grad = (grad + got[...].astype(F32)).astype(BF)
        keep_a[...] = grad[:q]
        send_a[...] = grad[q : 2 * q]
        if high:
            send_b[...] = grad[2 * q :]
        else:
            keep_b[...] = grad[2 * q :]

    @pl.when(j < half)
    def _():
        go(r0, False)

    @pl.when(j >= half)
    def _():
        go(r1, True)


def weight_cols(left, r0, r1, got=None, deps=()):
    tokens, k = left.shape
    n = r0.shape[1]
    block = 512
    half = n // block
    low = pl.BlockSpec((tokens, block), lambda j: (0, jnp.minimum(j, half - 1)))
    high = pl.BlockSpec((tokens, block), lambda j: (0, jnp.maximum(j - half, 0)))
    full = pl.BlockSpec((k, block), lambda j: (0, j))
    outs, out_specs, more = [jax.ShapeDtypeStruct((k, 2 * n), BF)], [full], []
    if got is not None:
        a = jax.ShapeDtypeStruct((k // 4, 2 * n), BF)
        b = jax.ShapeDtypeStruct((k // 2, n), BF)
        outs = [a, a, b, b]
        sa = pl.BlockSpec((k // 4, block), lambda j: (0, j))
        out_specs = [
            sa,
            sa,
            pl.BlockSpec((k // 2, block), lambda j: (0, jnp.minimum(j, half - 1))),
            pl.BlockSpec((k // 2, block), lambda j: (0, jnp.maximum(j - half, 0))),
        ]
        more = [got]
    return kernel(
        functools.partial(cols_body, half=half, added=got is not None),
        "weight_cols",
        (2 * half,),
        [whole_of(left), low, high] + [full] * len(more),
        out_specs,
        outs,
        (left, r0, r1, *more,),
        scratch=[pltpu.VMEM((k, tokens), BF)],
        deps=deps,
    )


class Order:
    def __init__(self):
        self.token = jnp.zeros((8, 128), F32)

    def at(self, *values):
        values, self.token = lax.optimization_barrier((values, self.token))
        return values if len(values) > 1 else values[0]


def rows_cat(*parts):
    return jnp.concatenate(parts, axis=0)


def one_sequence(
    stream, lengths, assignment, cotangent, w_qkv, b_qv, w_out, w_in, b_in, w_back, gains, shifts
):
    _, own, width = stream.shape
    rows = 2 * own
    dp = lax.axis_size("dp")
    x = lax.axis_index("tensor")
    spot = lax.axis_index("dp")
    zi, yi, ci = spot // 4, (spot // 2) % 2, spot % 2
    lanes = 128

    order = Order()
    at = order.at
    routes = {
        "x": ("tensor", [(0, 1), (1, 0)]),
        "y": ("dp", [(i, i ^ 2) for i in range(dp)]),
        "c": ("dp", [(i, i ^ 1) for i in range(dp)]),
    }
    for k in range(1, 4):
        routes[k] = ("dp", [(i, (i + 4 * k) % dp) for i in range(dp)])
        routes[-k] = ("dp", [(i, (i - 4 * k) % dp) for i in range(dp)])

    def send(way, value):
        return lax.ppermute(at(value), *routes[way])

    def along_z(value):
        value = at(value)
        return [lax.ppermute(value, *routes[k]) for k in range(1, 4)]

    def other(v):
        return lax.dynamic_index_in_dim(v, 1 - x, 0, keepdims=False)

    def mine(v):
        return lax.dynamic_index_in_dim(v, x, 0, keepdims=False)

    n = jnp.arange(dp, dtype=jnp.int32)
    slot = (zi - n // 4) % 4
    first_half = slot < 2
    y_rel = (n // 2) % 2 ^ yi
    c_rel = n % 2 ^ ci
    k2 = slot % 2
    col_place = (slot // 2) * 4 + y_rel * 2 + k2

    def row_place(x_rel):
        return jnp.where(first_half, y_rel * 4 + x_rel * 2 + k2, 8 + x_rel * 4 + y_rel * 2 + k2)

    def one_hot(dest, size):
        return (dest[:, None] == jnp.arange(size, dtype=jnp.int32)[None, :]).astype(BF)

    def spread(block_dest, block):
        count = block_dest.shape[0]
        dest = block_dest[:, None] * block + jnp.arange(block, dtype=jnp.int32)[None, :]
        return one_hot(dest.reshape(-1), count * block)

    perm_in = spread(c_rel * (dp // 2) + col_place, width // dp)
    perm_ctx = spread(
        jnp.concatenate([c_rel * dp + row_place(0), c_rel * dp + row_place(1)]), width // (2 * dp)
    )
    place = x[None].astype(jnp.int32)

    def lane_rows(v):
        v = v.astype(BF)
        return jnp.pad(v, ((0, 0), (0, lanes - v.shape[1])))

    small = jnp.concatenate(
        [
            b_in.reshape(1, lanes),
            lane_rows(gains.T),
            lane_rows(shifts.T),
            lane_rows(b_qv.T),
            jnp.zeros((7, lanes), BF),
        ],
        axis=0,
    )

    def add(u, v):
        return u.astype(F32) + v.astype(F32)

    groups = width // 2 // lanes
    hw = width // 2
    qs = w_qkv.reshape(-1, 3, groups, lanes).transpose(0, 2, 1, 3).reshape(-1, 3 * hw)

    count = jnp.sum(lengths).astype(F32)
    all_seqs = lengths.shape[0]
    matches = mine(assignment) == jnp.arange(all_seqs, dtype=jnp.int32)
    slot_len = jnp.sum(jnp.where(matches, lengths, 0))
    info = jnp.stack([slot_len, x]).astype(jnp.int32)
    row = jnp.arange(rows, dtype=jnp.int32)
    position = jnp.where(row < own, row + x * own, row - x * own)
    factor = F32(all_seqs * rows) / count
    live = jnp.where(position < slot_len, factor, 0.0)
    info, live, perm_in, perm_ctx, place, rel_at = (
        info,
        live,
        perm_in,
        perm_ctx,
        place,
        one_hot(c_rel * 8 + y_rel * 4 + slot, dp),
    )

    dw = width // dp
    bw = width // (2 * dp)

    def unpack(sm):
        sm = sm.transpose(0, 1, 3, 2, 4, 5).reshape(dp, 2, 16, lanes)
        sm = jnp.einsum("nr,rxql->nxql", rel_at, sm, preferred_element_type=F32)
        vecs = sm[:, 0, 1:9, :dw].transpose(1, 0, 2).reshape(8, width)
        bias_up = sm[:, :, 0].transpose(1, 0, 2).reshape(1, -1)
        bias = sm[:, :, 7:9, :bw].transpose(2, 1, 0, 3).reshape(2, 2, groups, 1, lanes)
        bias = jnp.concatenate([bias[0], jnp.zeros_like(bias[0]), bias[1]], axis=2)
        return vecs, bias_up, bias.reshape(1, -1)

    q1, q2, q3 = along_z(qs)
    theirs = send("x", other(stream))
    t1, t2, t3 = along_z(small)
    q1, q2, q3 = at(q1, q2, q3)
    qa, qb = rows_cat(qs, q1), rows_cat(q2, q3)
    qax, qby = send("x", qa), send("y", qb)
    o1, o2, o3 = along_z(w_out)
    t1, t2, t3 = at(t1, t2, t3)
    sm = jnp.stack([small, t1, t2, t3])
    tx = send("x", sm)
    theirs = at(theirs)
    own_seq = rows_cat(mine(stream), theirs)
    stream_rel = dot(own_seq, perm_in).astype(BF)
    i1, i2, i3 = along_z(w_in)
    wb = lax.all_gather(at(w_back), ("tensor", "dp"), axis=0, tiled=True)
    qax, qby = at(qax, qby)
    qay, qaxy, qbx, qbxy = send("y", qa), send("y", qax), send("x", qb), send("x", qby)
    tx = at(tx)
    sm = jnp.stack([sm, tx])
    ty = send("y", sm)
    o1, o2, o3 = at(o1, o2, o3)
    oa, ob = rows_cat(w_out, o1), rows_cat(o2, o3)
    ty = at(ty)
    sm = jnp.stack([sm, ty])
    tc = send("c", sm)
    qay, qbx = at(qay, qbx)
    q00 = rows_cat(qa, qay, qb, qby)
    q10 = send("c", q00)
    qaxy, qbxy = at(qaxy, qbxy)
    q01 = rows_cat(qax, qaxy, qbx, qbxy)
    q11 = send("c", q01)
    oax, oby = send("x", oa), send("y", ob)
    tc = at(tc)
    vecs, bias_up, bias_proj = unpack(jnp.stack([sm, tc]))
    i1, i2, i3 = at(i1, i2, i3)
    ia, ib = rows_cat(w_in, i1), rows_cat(i2, i3)
    iax, iby = send("x", ia), send("y", ib)
    q10, q11, bias_proj, vecs, bias_up = at(q10, q11, bias_proj, vecs, bias_up)
    wq = [[q00, q01], [q10, q11]]
    proj = at(project(at(stream_rel), wq, bias_proj, 3 * lanes))
    oax, oby, iax, iby = at(oax, oby, iax, iby)
    oay, oaxy, obx, obxy = send("y", oa), send("y", oax), send("x", ob), send("x", oby)
    iay, ibx = send("y", ia), send("x", ib)
    ctx0 = at(attend(info, at(proj), lanes, 0))
    oay, oaxy, obx, obxy, iay, ibx = at(oay, oaxy, obx, obxy, iay, ibx)
    wo0 = rows_cat(oa, oax, oay, oaxy, ob, oby, obx, obxy)
    wo1 = send("c", wo0)
    iaxy, ibxy = send("y", iax), send("x", iby)
    ctx1 = at(attend(info, at(proj), lanes, 1))
    wo1, iaxy, ibxy = at(wo1, iaxy, ibxy)
    i00, i01 = rows_cat(ia, iay, ib, iby), rows_cat(iax, iaxy, ibx, ibxy)
    i10, i11 = send("c", i00), send("c", i01)
    tile = own // 2
    zhat1, r1, mixed, mixed_rel, ctx_rel = mix(
        at(ctx0), ctx1, own_seq, wo0, wo1, perm_ctx, perm_in, vecs, tile
    )
    i10, i11, mixed_rel = at(i10, i11, mixed_rel)
    cot_theirs = send("x", other(cotangent))
    wi = [[i00, i01], [i10, i11]]
    block = 2 * lanes
    hidden, slope = up_gelu(at(mixed_rel), wi, bias_up, place, block)
    hidden, cot_theirs, wb = at(hidden, cot_theirs, wb)
    cot = rows_cat(mine(cotangent), cot_theirs)
    live = jnp.broadcast_to(live[:, None], (rows, lanes))
    result, grad_sum2, grad_branch, sums2 = turn(hidden, wb, mixed, cot, live, vecs, tile)

    def whole(both, got):
        return jnp.where(x == 0, jnp.stack([both, got]), jnp.stack([got, both]))

    def finish(a, b, n):
        parts = a[n:].astype(BF), b[:n].astype(BF), b[n:].astype(BF)
        got = [lax.ppermute(v, *routes[-1 - i]) for i, v in enumerate(parts)]
        return lambda: add(a[:n], got[0]) + add(got[1], got[2])

    def join(a_near, a_far, b_near, b_far, a, b):
        a1, b1 = add(a_far, a[1]).astype(BF), add(b_far, b[1]).astype(BF)
        got = send("x", a1), send("y", b1)
        return got, add(a_near, a[0]), add(b_near, b[0]), a1

    def half_rows(v):
        e = v.shape[0] // 2
        return v[:e], v[e:]

    def half_cols(v):
        e = v.shape[1] // 2
        return v[:, :e], v[:, e:]

    def join_rows(keep_a, keep_b, a, b):
        return join(*half_rows(keep_a), *half_rows(keep_b), half_rows(a), half_rows(b))

    def join_cols(keep_a, keep_b, a, b):
        return join(*half_cols(keep_a), *half_rows(keep_b), half_cols(a), half_rows(b))

    def joined(got, a, b, _, n):
        got = at(*got)
        return add(a, got[0]), add(b, got[1]), n

    grad_branch, hidden = at(grad_branch, hidden)
    back = dot(hidden, grad_branch, TN).astype(BF)
    back_done = lax.psum_scatter(at(back), ("tensor", "dp"), scatter_dimension=0, tiled=True)
    lo_theirs = send("x", result[own:])
    di0, us0 = down_grad(at(grad_branch), wb, slope, place, block, 0)
    di1, us1 = down_grad(at(grad_branch), wb, slope, place, block, 1)
    di0, di1 = at(di0, di1)
    m0, m1 = half_cols(mixed_rel)
    i_core = jnp.concatenate([dot(m1, r, TN).astype(BF) for r in (di0, di1)], axis=1)
    i_got = send("c", i_core)
    grad_sum1, grad_att, grad_ctx, sums1 = unmix(
        at(di0), di1, wi, perm_in, grad_sum2, zhat1, r1, wo0, wo1, perm_ctx, vecs, own, deps=[i_core]
    )
    grad_att, i_got = at(grad_att, i_got)
    ik_a, is_a, ik_b, is_b = weight_cols(m0, di0, di1, i_got, deps=[grad_att])
    ia_got, ib_got = send("y", is_a), send("x", is_b)
    c0, c1 = half_cols(ctx_rel)
    o_core = dot(c1, grad_att, TN).astype(BF)
    o_got = send("c", o_core)
    dp0, ps0 = attend_grad(info, proj, at(grad_ctx), lanes, 0, deps=[is_a, o_core])
    dp0, o_got = at(dp0, o_got)
    ok_a, os_a, ok_b, os_b = weight_rows(c0, grad_att, o_got, deps=[dp0])
    oa_got, ob_got = send("y", os_a), send("x", os_b)
    dp1, ps1 = attend_grad(info, proj, at(grad_ctx), lanes, 1, deps=[os_a])
    dp1 = at(dp1)
    s0, s1 = half_cols(stream_rel)
    q_core = jnp.concatenate([dot(s1, r, TN).astype(BF) for r in (dp0, dp1)], axis=1)
    q_got = send("c", q_core)
    ia_got, ib_got, oa_got, ob_got = at(ia_got, ib_got, oa_got, ob_got)
    i_join = join_cols(ik_a, ik_b, ia_got, ib_got)
    o_join = join_rows(ok_a, ok_b, oa_got, ob_got)
    qk_a, qs_a, qk_b, qs_b = weight_cols(s0, dp0, dp1, at(q_got), deps=[i_join[3], o_join[3]])
    qa_got, qb_got = send("y", qs_a), send("x", qs_b)
    grad_stream = stream_grad(dp0, dp1, wq, perm_in, grad_sum1, own, deps=[qs_a])
    grad_stream, qa_got, qb_got = at(grad_stream, qa_got, qb_got)
    q_join = join_cols(qk_a, qk_b, qa_got, qb_got)
    in_done = finish(*joined(*i_join, w_in.shape[0]))
    out_done = finish(*joined(*o_join, w_out.shape[0]))
    gs_theirs = send("x", grad_stream[own:])
    qkv_done = finish(*joined(*q_join, qs.shape[0]))

    proj_sum = jnp.concatenate([ps0, ps1], axis=1).reshape(2, groups, 3, lanes)
    bias_grad = [proj_sum[:, :, j].reshape(2, dp, bw).transpose(1, 0, 2) for j in (0, 2)]
    up_sum = jnp.concatenate([us0, us1], axis=1)

    def widen(v):
        return jnp.pad(v, ((0, 0), (0, 0), (0, lanes - v.shape[2])))

    def both_halves(v):
        return jnp.broadcast_to(widen(v.reshape(dp, 1, dw)), (dp, 2, lanes))

    tiny = [up_sum.reshape(2, dp, lanes).transpose(1, 0, 2)]
    tiny += [both_halves(v) for v in (sums1[0], sums2[0], sums1[1], sums1[2], sums2[1], sums2[2])]
    tiny += [widen(v) for v in bias_grad]
    tiny += [jnp.zeros_like(tiny[0])] * 7
    tiny = jnp.stack(tiny, axis=2)
    tiny = jnp.einsum(
        "nr,nxql->rxql", rel_at.astype(F32), tiny, precision=lax.Precision.HIGHEST
    ).reshape(2, 2, 4, 2, 16, lanes)

    tiny = tiny[0] + send("c", tiny[1].astype(BF)).astype(F32)
    tiny = tiny[0] + send("y", tiny[1].astype(BF)).astype(F32)
    tiny = tiny[:, 0] + send("x", tiny[:, 1].astype(BF)).astype(F32)
    t = finish(tiny[:2], tiny[2:], 1)()[0]
    layer_out = whole(result[:own], lo_theirs)
    grad_stream = whole(grad_stream[:own], gs_theirs)

    return (
        layer_out,
        grad_stream,
        qkv_done().reshape(-1, groups, 3, lanes).transpose(0, 2, 1, 3).reshape(w_qkv.shape),
        t[7:9, :bw].T,
        out_done(),
        in_done(),
        t[0],
        back_done.astype(F32),
        t[1:3, :dw].T,
        t[3:7, :dw].T,
    )


def solution(mesh):
    in_specs = (
        P("dp", "tensor", None),
        P(),
        P("dp"),
        P("dp", "tensor", None),
        P("dp", None, "tensor"),
        P(("tensor", "dp"), None),
        P(("tensor", "dp"), None),
        P("dp", "tensor"),
        P(("tensor", "dp")),
        P(("tensor", "dp"), None),
        P("dp", None),
        P("dp", None),
    )
    out_specs = (
        P("dp", "tensor", None),
        P("dp", "tensor", None),
        P("dp", None, "tensor"),
        P(("tensor", "dp"), None),
        P(("tensor", "dp"), None),
        P("dp", "tensor"),
        P(("tensor", "dp")),
        P(("tensor", "dp"), None),
        P("dp", None),
        P("dp", None),
    )
    here = dict(mesh.shape)
    paired = here["tensor"] == 2 and here["dp"] == 16
    return jax.shard_map(
        one_sequence if paired else per_device, mesh=mesh, in_specs=in_specs, out_specs=out_specs, check_vma=False
    )
```

```python
import functools

import jax
import jax.numpy as jnp
from jax import lax
from jax.experimental import pallas as pl
from jax.experimental.pallas import tpu as pltpu
from jax.sharding import PartitionSpec as P

HD = 64
BF = jnp.bfloat16
F32 = jnp.float32
VMEM = 56 * 1024 * 1024


def norm_rows(summed, gain, offset):
    centred = summed - jnp.mean(summed, axis=-1, keepdims=True)
    variance = jnp.mean(centred * centred, axis=-1, keepdims=True)
    return centred * lax.rsqrt(variance + 1e-06) * gain + offset


def exact_gelu(values):
    return jax.nn.gelu(values, approximate=False)


def per_device(
    stream, lengths, assignment, cotangent, w_qkv, b_qv, w_out, w_in, b_in, w_back, gains, shifts
):
    count = jnp.sum(lengths).astype(jnp.float32)
    all_seqs = lengths.shape[0]
    matches = assignment[:, None] == jnp.arange(all_seqs, dtype=jnp.int32)[None, :]
    slot_len = jnp.sum(jnp.where(matches, lengths[None, :], 0), axis=1)
    (
        projection_weight,
        mixing_weight,
        up_weight,
        down_weight,
        bias_qv,
        bias_up,
        gain_all,
        shift_all,
    ) = (
        lax.all_gather(w_qkv, "dp", axis=0, tiled=True),
        lax.all_gather(w_out, "dp", axis=0, tiled=True),
        lax.all_gather(w_in, "dp", axis=0, tiled=True),
        lax.all_gather(w_back, "dp", axis=0, tiled=True),
        lax.all_gather(b_qv, "dp", axis=0, tiled=True),
        lax.all_gather(b_in, "dp", axis=0, tiled=True),
        lax.all_gather(gains, "dp", axis=0, tiled=True),
        lax.all_gather(shifts, "dp", axis=0, tiled=True),
    )
    seqs_dev, rows_dev, width = stream.shape
    full_rows = rows_dev * lax.axis_size("tensor")
    local_width = projection_weight.shape[2]
    shape_heads = (seqs_dev, full_rows, local_width // HD, HD)
    scale = HD ** (-0.5)
    gain_f = gain_all.astype(jnp.float32)
    shift_f = shift_all.astype(jnp.float32)
    bias_f = bias_qv.astype(jnp.float32)
    gathered_rows = lax.all_gather(stream, "tensor", axis=1, tiled=True)
    projected_rows = jnp.einsum(
        "bpo,orn->bprn", gathered_rows, projection_weight, preferred_element_type=jnp.float32
    )
    queries = (projected_rows[:, :, 0] + bias_f[:, 0]).astype(jnp.bfloat16).reshape(shape_heads)
    key_rows = projected_rows[:, :, 1].astype(jnp.bfloat16).reshape(shape_heads)
    value_rows = (projected_rows[:, :, 2] + bias_f[:, 1]).astype(jnp.bfloat16).reshape(shape_heads)
    allowed = jnp.arange(full_rows, dtype=jnp.int32)[None, :] < slot_len[:, None]
    products = jnp.einsum("sqhe,skhe->shqk", queries, key_rows, preferred_element_type=jnp.float32)
    scores = jnp.where(allowed[:, None, None, :], products * scale, -1e30)
    highest_score = jnp.max(scores, axis=-1, keepdims=True)
    expo = jnp.exp(scores - highest_score)
    weights = expo / jnp.sum(expo, axis=-1, keepdims=True)
    weights_low = weights.astype(jnp.bfloat16)
    context_rows = jnp.einsum(
        "shqk,skhe->sqhe", weights_low, value_rows, preferred_element_type=jnp.float32
    )
    context_rows = context_rows.reshape(seqs_dev, full_rows, local_width).astype(jnp.bfloat16)
    attention_terms = jnp.einsum(
        "kqz,zw->kqw", context_rows, mixing_weight, preferred_element_type=jnp.float32
    )
    attended = (
        lax.psum_scatter(
            attention_terms.astype(jnp.bfloat16), "tensor", scatter_dimension=1, tiled=True
        ).astype(jnp.float32)
        + shift_f[:, 1]
    )
    mixed, first_pull = jax.vjp(
        norm_rows, stream.astype(jnp.float32) + attended, gain_f[:, 0], shift_f[:, 0]
    )
    mixed_every_row = lax.all_gather(mixed.astype(jnp.bfloat16), "tensor", axis=1, tiled=True)
    inner = jnp.einsum(
        "vrw,wy->vry", mixed_every_row, up_weight, preferred_element_type=jnp.float32
    ) + bias_up.astype(jnp.float32)
    hidden, gelu_pull = jax.vjp(exact_gelu, inner)
    hidden_reduced = hidden.astype(jnp.bfloat16)
    perceptron_terms = jnp.einsum(
        "kqz,zw->kqw", hidden_reduced, down_weight, preferred_element_type=jnp.float32
    )
    branch = (
        lax.psum_scatter(
            perceptron_terms.astype(jnp.bfloat16), "tensor", scatter_dimension=1, tiled=True
        ).astype(jnp.float32)
        + shift_f[:, 3]
    )
    result, second_pull = jax.vjp(norm_rows, mixed + branch, gain_f[:, 1], shift_f[:, 2])
    position = lax.axis_index("tensor") * rows_dev + jnp.arange(rows_dev, dtype=jnp.int32)
    live = (position[None, :] < slot_len[:, None]).astype(jnp.float32)
    factor = jnp.float32(seqs_dev * lax.axis_size("dp") * full_rows) / count
    seed_grad = cotangent.astype(jnp.float32) * live[:, :, None] * factor
    grad_sum2, grad_gain2, grad_shift2 = second_pull(seed_grad)
    grad_branch = grad_sum2.astype(jnp.bfloat16)
    branch_bias_grad = jnp.sum(grad_branch.astype(jnp.float32), axis=(0, 1))
    branch_every_row = lax.all_gather(grad_branch, "tensor", axis=1, tiled=True)
    down_part = jnp.einsum(
        "irk,irt->kt", hidden_reduced, branch_every_row, preferred_element_type=jnp.float32
    )
    hidden_gradient = jnp.einsum(
        "atj,gj->atg", branch_every_row, down_weight, preferred_element_type=jnp.float32
    )
    inner_gradient = gelu_pull(hidden_gradient)[0].astype(jnp.bfloat16)
    up_bias_part = jnp.sum(inner_gradient.astype(jnp.float32), axis=(0, 1))
    up_portion = jnp.einsum(
        "pna,pnb->ab", mixed_every_row, inner_gradient, preferred_element_type=jnp.float32
    )
    mixed_partial_terms = jnp.einsum(
        "yjc,oc->yjo", inner_gradient, up_weight, preferred_element_type=jnp.float32
    )
    grad_mixed = grad_sum2 + lax.psum_scatter(
        mixed_partial_terms.astype(jnp.bfloat16), "tensor", scatter_dimension=1, tiled=True
    ).astype(jnp.float32)
    grad_sum1, grad_gain1, grad_shift1 = first_pull(grad_mixed)
    grad_attended = grad_sum1.astype(jnp.bfloat16)
    mix_bias_grad = jnp.sum(grad_attended.astype(jnp.float32), axis=(0, 1))
    attended_every_row = lax.all_gather(grad_attended, "tensor", axis=1, tiled=True)
    mixing_portion = jnp.einsum(
        "irk,irt->kt", context_rows, attended_every_row, preferred_element_type=jnp.float32
    )
    grad_context = jnp.einsum(
        "atj,gj->atg", attended_every_row, mixing_weight, preferred_element_type=jnp.float32
    )
    grad_context = grad_context.astype(jnp.bfloat16).reshape(shape_heads)
    grad_values = jnp.einsum(
        "shqk,sqhe->skhe", weights_low, grad_context, preferred_element_type=jnp.float32
    ).astype(jnp.bfloat16)
    grad_weights = jnp.einsum(
        "sqhe,skhe->shqk", grad_context, value_rows, preferred_element_type=jnp.float32
    )
    grad_scores = weights * (grad_weights - jnp.sum(weights * grad_weights, axis=-1, keepdims=True))
    grad_products = (grad_scores * scale).astype(jnp.bfloat16)
    grad_queries = jnp.einsum(
        "shqk,skhe->sqhe", grad_products, key_rows, preferred_element_type=jnp.float32
    ).astype(jnp.bfloat16)
    grad_keys = jnp.einsum(
        "shqk,sqhe->skhe", grad_products, queries, preferred_element_type=jnp.float32
    ).astype(jnp.bfloat16)
    flat_shape = (seqs_dev, full_rows, local_width)
    projection_gradient = jnp.stack(
        [
            grad_queries.reshape(flat_shape),
            grad_keys.reshape(flat_shape),
            grad_values.reshape(flat_shape),
        ],
        axis=2,
    )
    proj_bias_part = jnp.stack(
        [
            jnp.sum(grad_queries.astype(jnp.float32).reshape(flat_shape), axis=(0, 1)),
            jnp.sum(grad_values.astype(jnp.float32).reshape(flat_shape), axis=(0, 1)),
        ],
        axis=1,
    )
    projection_portion = jnp.einsum(
        "tqj,tquk->juk", gathered_rows, projection_gradient, preferred_element_type=jnp.float32
    )
    stream_terms = jnp.einsum(
        "wvjo,xjo->wvx", projection_gradient, projection_weight, preferred_element_type=jnp.float32
    )
    grad_stream = grad_sum1 + lax.psum_scatter(
        stream_terms.astype(jnp.bfloat16), "tensor", scatter_dimension=1, tiled=True
    ).astype(jnp.float32)
    gain_part = jnp.stack([grad_gain1, grad_gain2], axis=1)
    shift_part = jnp.stack([grad_shift1, mix_bias_grad, grad_shift2, branch_bias_grad], axis=1)
    proj_done, proj_bias_done, mix_done, up_done, up_bias_done, down_done, gain_done, shift_done = (
        lax.psum_scatter(
            projection_portion.astype(jnp.bfloat16), "dp", scatter_dimension=0, tiled=True
        ).astype(jnp.float32),
        lax.psum_scatter(
            proj_bias_part.astype(jnp.bfloat16), "dp", scatter_dimension=0, tiled=True
        ).astype(jnp.float32),
        lax.psum_scatter(
            mixing_portion.astype(jnp.bfloat16), "dp", scatter_dimension=0, tiled=True
        ).astype(jnp.float32),
        lax.psum_scatter(
            up_portion.astype(jnp.bfloat16), "dp", scatter_dimension=0, tiled=True
        ).astype(jnp.float32),
        lax.psum_scatter(
            up_bias_part.astype(jnp.bfloat16), "dp", scatter_dimension=0, tiled=True
        ).astype(jnp.float32),
        lax.psum_scatter(
            down_part.astype(jnp.bfloat16), "dp", scatter_dimension=0, tiled=True
        ).astype(jnp.float32),
        lax.psum_scatter(
            gain_part.astype(jnp.bfloat16), "dp", scatter_dimension=0, tiled=True
        ).astype(jnp.float32),
        lax.psum_scatter(
            shift_part.astype(jnp.bfloat16), "dp", scatter_dimension=0, tiled=True
        ).astype(jnp.float32),
    )
    gain_total, shift_total = lax.psum((gain_done, shift_done), "tensor")
    return (
        result.astype(jnp.bfloat16),
        grad_stream.astype(jnp.bfloat16),
        proj_done,
        proj_bias_done,
        mix_done,
        up_done,
        up_bias_done,
        down_done,
        gain_total,
        shift_total,
    )


def kernel(body, name, grid, in_specs, out_specs, out_shape, args, *, scratch=(), prefetch=0, deps=()):
    inputs = prefetch + len(in_specs)

    def without_deps(*refs):
        body(*refs[:inputs], *refs[inputs + len(deps) :])

    return pl.pallas_call(
        without_deps,
        grid_spec=pltpu.PrefetchScalarGridSpec(
            num_scalar_prefetch=prefetch,
            grid=grid,
            in_specs=list(in_specs) + [pl.BlockSpec(memory_space=pl.ANY)] * len(deps),
            out_specs=out_specs,
            scratch_shapes=scratch,
        ),
        out_shape=out_shape,
        compiler_params=pltpu.CompilerParams(vmem_limit_bytes=VMEM),
        name=name,
    )(*args, *deps)


def gelu_terms(v):
    density = jnp.exp(v * v * -0.5)
    t = 1.0 / (1.0 + (0.3275911 * 0.7071067811865476) * jnp.abs(v))
    poly = t * (
        0.254829592
        + t * (-0.284496736 + t * (1.421413741 + t * (-1.453152027 + t * 1.061405429)))
    )
    tail = 0.5 * poly * density
    return jnp.where(v >= 0, 1.0 - tail, tail), density * 0.3989422804014327


def dot(a, b, dims=((1,), (0,))):
    return lax.dot_general(a, b, (dims, ((), ())), preferred_element_type=F32)


def project_body(a_ref, w00, w10, w01, w11, b_ref, o_ref, *, half):
    j = pl.program_id(0)
    k = w00.shape[0]

    def go(w0, w1):
        acc = dot(a_ref[:, :k], w0[...]) + dot(a_ref[:, k:], w1[...]) + b_ref[...]
        o_ref[...] = acc.astype(o_ref.dtype)

    @pl.when(j < half)
    def _():
        go(w00, w10)

    @pl.when(j >= half)
    def _():
        go(w01, w11)


def split_specs(rows, block, half):
    low = pl.BlockSpec((rows, block), lambda j, *_: (0, jnp.minimum(j, half - 1)))
    high = pl.BlockSpec((rows, block), lambda j, *_: (0, jnp.maximum(j - half, 0)))
    return [low, low, high, high]


def project(a, w, bias, block, deps=()):
    rows, width = a.shape
    cols = w[0][0].shape[1]
    half = cols // block
    return kernel(
        functools.partial(project_body, half=half),
        "project",
        (2 * half,),
        [pl.BlockSpec((rows, width), lambda j: (0, 0))]
        + split_specs(width // 2, block, half)
        + [pl.BlockSpec((1, block), lambda j: (0, j))],
        pl.BlockSpec((rows, block), lambda j: (0, j)),
        jax.ShapeDtypeStruct((rows, 2 * cols), BF),
        (a, w[0][0], w[1][0], w[0][1], w[1][1], bias,),
        deps=deps,
    )


def up_body(a_ref, w_ref, b_ref, h_ref, g_ref, acc):
    new = dot(a_ref[...], w_ref[...])
    v = acc[...]
    cdf, density = gelu_terms(v)
    h_ref[...] = (v * cdf).astype(BF)
    g_ref[...] = (cdf + v * density).astype(BF)
    acc[...] = new + b_ref[...]


def up_gelu(a, w, bias, block, deps=()):
    rows, width = a.shape
    cols = w.shape[1]
    end = cols // block - 1
    out = jax.ShapeDtypeStruct((rows, cols), BF)
    spot = pl.BlockSpec((rows, block), lambda j: (0, jnp.maximum(j - 1, 0)))
    return kernel(
        up_body,
        "up_gelu",
        (end + 2,),
        [
            whole_of(a),
            pl.BlockSpec((width, block), lambda j: (0, jnp.minimum(j, end))),
            pl.BlockSpec((1, block), lambda j: (0, jnp.minimum(j, end))),
        ],
        [spot, spot],
        [out, out],
        (a, w, bias),
        scratch=[pltpu.VMEM((rows, block), F32)],
        deps=deps,
    )


def matmul_body(a_ref, w_ref, o_ref):
    o_ref[...] = dot(a_ref[...], w_ref[...]).astype(o_ref.dtype)


def matmul(a, w, block, dtype, deps=()):
    return kernel(
        matmul_body,
        "matmul",
        (w.shape[1] // block,),
        [whole_of(a), pl.BlockSpec((w.shape[0], block), lambda j: (0, j))],
        pl.BlockSpec((a.shape[0], block), lambda j: (0, j)),
        jax.ShapeDtypeStruct((a.shape[0], w.shape[1]), dtype),
        (a, w),
        deps=deps,
    )


def down_grad_body(a_ref, w_ref, g_ref, d_ref, s_ref):
    d = dot(a_ref[...], w_ref[...], ((1,), (1,)))
    d = (d * g_ref[...].astype(F32)).astype(BF)
    d_ref[...] = d
    s_ref[...] = jnp.sum(d.astype(F32), axis=0, keepdims=True)


def down_grad(a, w, g, block, deps=()):
    rows, width = a.shape
    cols = g.shape[1]
    return kernel(
        down_grad_body,
        "down_grad",
        (cols // block,),
        [
            whole_of(a),
            pl.BlockSpec((block, width), lambda j: (j, 0)),
            pl.BlockSpec((rows, block), lambda j: (0, j)),
        ],
        [
            pl.BlockSpec((rows, block), lambda j: (0, j)),
            pl.BlockSpec((1, block), lambda j: (0, j)),
        ],
        [jax.ShapeDtypeStruct((rows, cols), BF), jax.ShapeDtypeStruct((1, cols), F32)],
        (a, w, g),
        deps=deps,
    )


def head_weights(info, q, k, rows):
    own = rows // 2
    at = lax.broadcasted_iota(jnp.int32, (1, rows), 1)
    first = info[1] * own
    pos = jnp.where(at < own, at + first, at - first)
    s = dot(q, k, ((1,), (1,)))
    s = jnp.where(pos < info[0], s * HD ** (-0.5), -1e30)
    e = jnp.exp(s - jnp.max(s, axis=1, keepdims=True))
    return e * (1.0 / jnp.sum(e, axis=1, keepdims=True))


def attend_body(info, p_ref, c_ref):
    rows, lanes = c_ref.shape
    for h in range(lanes // HD):
        part = [p_ref[:, j * lanes + h * HD : j * lanes + (h + 1) * HD] for j in range(3)]
        w = head_weights(info, part[0], part[1], rows).astype(BF)
        c_ref[:, h * HD : (h + 1) * HD] = dot(w, part[2]).astype(BF)


def attend_grad_body(info, p_ref, t_ref, d_ref, s_ref):
    rows, lanes = t_ref.shape
    tn = ((0,), (0,))
    for h in range(lanes // HD):
        q, k, v = [p_ref[:, j * lanes + h * HD : j * lanes + (h + 1) * HD] for j in range(3)]
        t = t_ref[:, h * HD : (h + 1) * HD]
        w = head_weights(info, q, k, rows)
        dw = dot(t, v, ((1,), (1,)))
        ds = w * (dw - jnp.sum(w * dw, axis=1, keepdims=True)) * HD ** (-0.5)
        ds = ds.astype(BF)
        outs = (dot(ds, k), dot(ds, q, tn), dot(w.astype(BF), t, tn))
        for j in range(3):
            at = slice(j * lanes + h * HD, j * lanes + (h + 1) * HD)
            low = outs[j].astype(BF)
            d_ref[:, at] = low
            s_ref[:, at] = jnp.sum(low.astype(F32), axis=0, keepdims=True)


def attend(info, proj, lanes, part, deps=()):
    rows, cols = proj.shape
    steps = cols // (6 * lanes)
    return kernel(
        attend_body,
        "attend",
        (steps,),
        [pl.BlockSpec((rows, 3 * lanes), lambda j, info: (0, j + part * steps))],
        pl.BlockSpec((rows, lanes), lambda j, info: (0, j)),
        jax.ShapeDtypeStruct((rows, cols // 6), BF),
        (info, proj,),
        prefetch=1,
        deps=deps,
    )


def attend_grad(info, proj, top, lanes, part, deps=()):
    rows, cols = proj.shape
    steps = cols // (6 * lanes)
    return kernel(
        attend_grad_body,
        "attend_grad",
        (steps,),
        [
                pl.BlockSpec((rows, 3 * lanes), lambda j, info: (0, j + part * steps)),
                pl.BlockSpec((rows, lanes), lambda j, info: (0, j + part * steps)),
            ],
        [
                pl.BlockSpec((rows, 3 * lanes), lambda j, info: (0, j)),
                pl.BlockSpec((1, 3 * lanes), lambda j, info: (0, j)),
            ],
        [
            jax.ShapeDtypeStruct((rows, cols // 2), BF),
            jax.ShapeDtypeStruct((1, cols // 2), F32),
        ],
        (info, proj, top,),
        prefetch=1,
        deps=deps,
    )


def whole_of(v):
    return pl.BlockSpec(v.shape, lambda *_: (0,) * v.ndim)


def tile_of(v, tile):
    return pl.BlockSpec((tile, v.shape[1]), lambda j: (j, 0))


def norm_of(z):
    centred = z - jnp.mean(z, axis=1, keepdims=True)
    r = lax.rsqrt(jnp.mean(centred * centred, axis=1, keepdims=True) + 1e-06)
    return centred * r, r


def norm_grad(t, zhat, r, gain):
    gt = t * gain
    mean = jnp.mean(gt, axis=1, keepdims=True)
    return r * (gt - mean - zhat * jnp.mean(gt * zhat, axis=1, keepdims=True))


def gather_sums(s_ref, *values):
    sums = [jnp.sum(v, axis=0, keepdims=True) for v in values]
    sums += [jnp.zeros_like(sums[0])] * (8 - len(sums))
    sums = jnp.concatenate(sums, axis=0)

    @pl.when(pl.program_id(0) == 0)
    def _():
        s_ref[...] = sums

    @pl.when(pl.program_id(0) != 0)
    def _():
        s_ref[...] += sums


def mix_body(c0, c1, s_ref, w0, w1, pc, v_ref, zh_ref, r_ref, m_ref, mr_ref, x_ref):
    h = w0.shape[0]
    ctx = dot(c0[...], pc[:h, :]) + dot(c1[...], pc[h:, :])
    ctx = ctx.astype(BF)
    x_ref[...] = ctx
    att = dot(ctx[:, :h], w0[...]) + dot(ctx[:, h:], w1[...]) + v_ref[3:4, :]
    zhat, r = norm_of(s_ref[...].astype(F32) + att)
    zh_ref[...] = zhat
    r_ref[...] = jnp.broadcast_to(r, r_ref.shape)
    mixed = zhat * v_ref[0:1, :] + v_ref[2:3, :]
    m_ref[...] = mixed
    mr_ref[...] = mixed.astype(BF)


def mix(c0, c1, stream, w0, w1, perm_ctx, vecs, tile, deps=()):
    rows, width = stream.shape
    full = jax.ShapeDtypeStruct((rows, width), F32)
    low = jax.ShapeDtypeStruct((rows, width), BF)
    outs = [full, jax.ShapeDtypeStruct((rows, 128), F32), full, low, low]
    return kernel(
        mix_body,
        "mix",
        (rows // tile,),
        [tile_of(v, tile) for v in (c0, c1, stream)]
        + [whole_of(v) for v in (w0, w1, perm_ctx, vecs)],
        [tile_of(v, tile) for v in outs],
        outs,
        (c0, c1, stream, w0, w1, perm_ctx, vecs,),
        deps=deps,
    )


def turn_body(p_ref, t_ref, m_ref, c_ref, l_ref, v_ref, o_ref, g_ref, gb_ref, s_ref):
    branch = p_ref[...] + t_ref[...].astype(F32) + v_ref[5:6, :]
    zhat, r = norm_of(m_ref[...] + branch)
    gain = v_ref[1:2, :]
    o_ref[...] = (zhat * gain + v_ref[4:5, :]).astype(BF)
    seed = c_ref[...].astype(F32) * l_ref[:, 0:1]
    g = norm_grad(seed, zhat, r, gain)
    g_ref[...] = g
    low = g.astype(BF)
    gb_ref[...] = low
    gather_sums(s_ref, seed * zhat, seed, low.astype(F32))


def turn(part, theirs, mixed, cot, live, vecs, tile, deps=()):
    rows, width = mixed.shape
    full = jax.ShapeDtypeStruct((rows, width), F32)
    low = jax.ShapeDtypeStruct((rows, width), BF)
    sums = jax.ShapeDtypeStruct((8, width), F32)
    tiled = (part, theirs, mixed, cot, live)
    return kernel(
        turn_body,
        "turn",
        (rows // tile,),
        [tile_of(v, tile) for v in tiled] + [whole_of(vecs)],
        [tile_of(v, tile) for v in (low, full, low)] + [whole_of(sums)],
        [low, full, low, sums],
        (*tiled, vecs),
        deps=deps,
    )


def unmix_body(p_ref, t_ref, g2, zh, r_ref, wo0, wo1, pc, v_ref, g1_ref, ga_ref, gc_ref, s_ref):
    nt = ((1,), (1,))
    grad = g2[...] + p_ref[...] + t_ref[...].astype(F32)
    zhat = zh[...]
    g1 = norm_grad(grad, zhat, r_ref[:, 0:1], v_ref[0:1, :])
    g1_ref[...] = g1
    low = g1.astype(BF)
    ga_ref[...] = low
    ctx = jnp.concatenate([dot(low, wo0[...], nt), dot(low, wo1[...], nt)], axis=1)
    gc_ref[...] = dot(ctx.astype(BF), pc[...], nt).astype(BF)
    gather_sums(s_ref, grad * zhat, grad, low.astype(F32))


def unmix(part, theirs, g2, zhat, r, wo0, wo1, perm_ctx, vecs, tile, deps=()):
    rows, width = g2.shape
    full = jax.ShapeDtypeStruct((rows, width), F32)
    low = jax.ShapeDtypeStruct((rows, width), BF)
    sums = jax.ShapeDtypeStruct((8, width), F32)
    tiled = (part, theirs, g2, zhat, r)
    fixed = (wo0, wo1, perm_ctx, vecs)
    return kernel(
        unmix_body,
        "unmix",
        (rows // tile,),
        [tile_of(v, tile) for v in tiled] + [whole_of(v) for v in fixed],
        [tile_of(v, tile) for v in (full, low, low)] + [whole_of(sums)],
        [full, low, low, sums],
        tiled + fixed,
        deps=deps,
    )


def stream_body(d0, d1, w00, w10, w01, w11, pi, g1, o_ref):
    nt = ((1,), (1,))
    parts = [
        dot(d0[...], u[...], nt) + dot(d1[...], v[...], nt) for u, v in ((w00, w01), (w10, w11))
    ]
    back = jnp.concatenate(parts, axis=1).astype(BF)
    o_ref[...] = (g1[...] + dot(back, pi[...], nt)).astype(BF)


def stream_grad(d0, d1, w, perm_in, g1, tile, deps=()):
    out = jax.ShapeDtypeStruct(g1.shape, BF)
    ws = (w[0][0], w[1][0], w[0][1], w[1][1])
    return kernel(
        stream_body,
        "stream_grad",
        (g1.shape[0] // tile,),
        [tile_of(d0, tile), tile_of(d1, tile)]
        + [whole_of(v) for v in ws + (perm_in,)]
        + [tile_of(g1, tile)],
        tile_of(out, tile),
        out,
        (d0, d1, *ws, perm_in, g1,),
        deps=deps,
    )


TN = ((0,), (0,))


def rows_body(l_ref, r_ref, *refs, added, per):
    grad = dot(l_ref[...], r_ref[...], TN)
    if not added:
        refs[0][...] = grad.astype(BF)
        return
    grad = (grad + refs[0][...].astype(F32)).astype(BF)
    j = pl.program_id(0)
    for i in range(4):

        @pl.when(j // per == i)
        def _():
            refs[1 + i][...] = grad


def weight_rows(left, right, got=None, deps=()):
    tokens, k = left.shape
    n = right.shape[1]
    per = 2 if k // 8 % 128 == 0 else 1
    block = k // (4 * per)
    row = pl.BlockSpec((block, n), lambda j: (j, 0))
    outs, out_specs, more = [jax.ShapeDtypeStruct((k, n), BF)], [row], []
    if got is not None:
        outs = [jax.ShapeDtypeStruct((k // 4, n), BF)] * 4
        out_specs = [
            pl.BlockSpec((block, n), lambda j, i=i: (jnp.clip(j - per * i, 0, per - 1), 0))
            for i in range(4)
        ]
        more = [got]
    return kernel(
        functools.partial(rows_body, added=got is not None, per=per),
        "weight_rows",
        (4 * per,),
        [pl.BlockSpec((tokens, block), lambda j: (0, j)), whole_of(right)]
        + [row] * len(more),
        out_specs,
        outs,
        (left, right, *more,),
        deps=deps,
    )


def cols_body(l_ref, r0, r1, *refs, half, added):
    j = pl.program_id(0)
    turned = refs[-1]

    @pl.when(j == 0)
    def _():
        turned[...] = l_ref[...].T

    def go(r, high):
        grad = dot(turned[...], r[...])
        if not added:
            refs[0][...] = grad.astype(BF)
            return
        got, keep_a, send_a, keep_b, send_b = refs[:5]
        q = grad.shape[0] // 4
        grad = (grad + got[...].astype(F32)).astype(BF)
        keep_a[...] = grad[:q]
        send_a[...] = grad[q : 2 * q]
        if high:
            send_b[...] = grad[2 * q :]
        else:
            keep_b[...] = grad[2 * q :]

    @pl.when(j < half)
    def _():
        go(r0, False)

    @pl.when(j >= half)
    def _():
        go(r1, True)


def weight_cols(left, r0, r1, got=None, deps=()):
    tokens, k = left.shape
    n = r0.shape[1]
    block = 512
    half = n // block
    low = pl.BlockSpec((tokens, block), lambda j: (0, jnp.minimum(j, half - 1)))
    high = pl.BlockSpec((tokens, block), lambda j: (0, jnp.maximum(j - half, 0)))
    full = pl.BlockSpec((k, block), lambda j: (0, j))
    outs, out_specs, more = [jax.ShapeDtypeStruct((k, 2 * n), BF)], [full], []
    if got is not None:
        a = jax.ShapeDtypeStruct((k // 4, 2 * n), BF)
        b = jax.ShapeDtypeStruct((k // 2, n), BF)
        outs = [a, a, b, b]
        sa = pl.BlockSpec((k // 4, block), lambda j: (0, j))
        out_specs = [
            sa,
            sa,
            pl.BlockSpec((k // 2, block), lambda j: (0, jnp.minimum(j, half - 1))),
            pl.BlockSpec((k // 2, block), lambda j: (0, jnp.maximum(j - half, 0))),
        ]
        more = [got]
    return kernel(
        functools.partial(cols_body, half=half, added=got is not None),
        "weight_cols",
        (2 * half,),
        [whole_of(left), low, high] + [full] * len(more),
        out_specs,
        outs,
        (left, r0, r1, *more,),
        scratch=[pltpu.VMEM((k, tokens), BF)],
        deps=deps,
    )


def tie_body(*refs):
    pass


def tie(values, deps=()):
    spot = pl.BlockSpec(memory_space=pl.ANY)
    return pl.pallas_call(
        tie_body,
        in_specs=[spot] * (len(values) + len(deps)),
        out_specs=[spot] * len(values),
        out_shape=[jax.ShapeDtypeStruct(v.shape, v.dtype) for v in values],
        input_output_aliases={i: i for i in range(len(values))},
        name="tie",
    )(*values, *deps)


class Order:
    def __init__(self):
        self.token = jnp.zeros((8, 128), F32)

    def at(self, *values):
        values, self.token = lax.optimization_barrier((values, self.token))
        return values if len(values) > 1 else values[0]


def rows_cat(*parts):
    return jnp.concatenate(parts, axis=0)


def one_sequence(
    stream, lengths, assignment, cotangent, w_qkv, b_qv, w_out, w_in, b_in, w_back, gains, shifts
):
    _, own, width = stream.shape
    rows = 2 * own
    dp = lax.axis_size("dp")
    x = lax.axis_index("tensor")
    spot = lax.axis_index("dp")
    zi, yi, ci = spot // 4, (spot // 2) % 2, spot % 2
    lanes = 128

    order = Order()
    at = order.at
    routes = {
        "x": ("tensor", [(0, 1), (1, 0)]),
        "y": ("dp", [(i, i ^ 2) for i in range(dp)]),
        "c": ("dp", [(i, i ^ 1) for i in range(dp)]),
    }
    for k in range(1, 4):
        routes[k] = ("dp", [(i, (i + 4 * k) % dp) for i in range(dp)])
        routes[-k] = ("dp", [(i, (i - 4 * k) % dp) for i in range(dp)])

    def send(way, value):
        return lax.ppermute(at(value), *routes[way])

    def along_z(value):
        value = at(value)
        return [lax.ppermute(value, *routes[k]) for k in range(1, 4)]

    def other(v):
        return lax.dynamic_index_in_dim(v, 1 - x, 0, keepdims=False)

    def mine(v):
        return lax.dynamic_index_in_dim(v, x, 0, keepdims=False)

    n = jnp.arange(dp, dtype=jnp.int32)
    slot = (zi - n // 4) % 4
    first_half = slot < 2
    y_rel = (n // 2) % 2 ^ yi
    c_rel = n % 2 ^ ci
    k2 = slot % 2
    col_place = (slot // 2) * 4 + y_rel * 2 + k2

    def row_place(x_rel):
        return jnp.where(first_half, y_rel * 4 + x_rel * 2 + k2, 8 + x_rel * 4 + y_rel * 2 + k2)

    def one_hot(dest, size):
        return (dest[:, None] == jnp.arange(size, dtype=jnp.int32)[None, :]).astype(BF)

    def spread(block_dest, block):
        count = block_dest.shape[0]
        dest = block_dest[:, None] * block + jnp.arange(block, dtype=jnp.int32)[None, :]
        return one_hot(dest.reshape(-1), count * block)

    perm_in = spread(c_rel * (dp // 2) + col_place, width // dp)
    perm_ctx = spread(
        jnp.concatenate([c_rel * dp + row_place(0), c_rel * dp + row_place(1)]), width // (2 * dp)
    )
    place = x[None].astype(jnp.int32)

    def lane_rows(v):
        v = v.astype(BF)
        return jnp.pad(v, ((0, 0), (0, lanes - v.shape[1])))

    small = jnp.concatenate(
        [
            b_in.reshape(1, lanes),
            lane_rows(gains.T),
            lane_rows(shifts.T),
            lane_rows(b_qv.T),
            jnp.zeros((7, lanes), BF),
        ],
        axis=0,
    )

    def add(u, v):
        return u.astype(F32) + v.astype(F32)

    groups = width // 2 // lanes
    hw = width // 2
    qs = w_qkv.reshape(-1, 3, groups, lanes).transpose(0, 2, 1, 3).reshape(-1, 3 * hw)

    count = jnp.sum(lengths).astype(F32)
    all_seqs = lengths.shape[0]
    matches = mine(assignment) == jnp.arange(all_seqs, dtype=jnp.int32)
    slot_len = jnp.sum(jnp.where(matches, lengths, 0))
    info = jnp.stack([slot_len, x]).astype(jnp.int32)
    row = jnp.arange(rows, dtype=jnp.int32)
    position = jnp.where(row < own, row + x * own, row - x * own)
    factor = F32(all_seqs * rows) / count
    live = jnp.where(position < slot_len, factor, 0.0)
    info, live, perm_in, perm_ctx, place, rel_at = (
        info,
        live,
        perm_in,
        perm_ctx,
        place,
        one_hot(c_rel * 8 + y_rel * 4 + slot, dp),
    )

    dw = width // dp
    bw = width // (2 * dp)

    def unpack(sm):
        sm = sm.transpose(0, 1, 3, 2, 4, 5).reshape(dp, 2, 16, lanes)
        sm = jnp.einsum("nr,rxql->nxql", rel_at, sm, preferred_element_type=F32)
        vecs = sm[:, 0, 1:9, :dw].transpose(1, 0, 2).reshape(8, width)
        bias_up = sm[:, 0, 0].reshape(1, -1)
        bias = sm[:, :, 7:9, :bw].transpose(2, 1, 0, 3).reshape(2, 2, groups, 1, lanes)
        bias = jnp.concatenate([bias[0], jnp.zeros_like(bias[0]), bias[1]], axis=2)
        return vecs, bias_up, bias.reshape(1, -1)

    q1, q2, q3 = along_z(qs)
    theirs = send("x", other(stream))
    t1, t2, t3 = along_z(small)
    q1, q2, q3, perm_in, perm_ctx = tie([q1, q2, q3, perm_in, perm_ctx], [theirs, t1, t2, t3])
    qa, qb = rows_cat(qs, q1), rows_cat(q2, q3)
    qax, qby = send("x", qa), send("y", qb)
    o1, o2, o3 = along_z(w_out)
    sm = jnp.stack([small, t1, t2, t3])
    tx = send("x", sm)
    theirs = at(theirs)
    own_seq = rows_cat(mine(stream), theirs)
    stream_rel = dot(own_seq, perm_in).astype(BF)
    in_shard, back_shard = tie([w_in, w_back], [q1, q2, q3])
    wi = lax.all_gather(in_shard, "dp", axis=0, tiled=True)
    wb = lax.all_gather(back_shard, "dp", axis=0, tiled=True)
    qax, qby = at(qax, qby)
    qay, qaxy, qbx, qbxy = send("y", qa), send("y", qax), send("x", qb), send("x", qby)
    tx = at(tx)
    sm = jnp.stack([sm, tx])
    ty = send("y", sm)
    o1, o2, o3 = at(o1, o2, o3)
    oa, ob = rows_cat(w_out, o1), rows_cat(o2, o3)
    ty = at(ty)
    sm = jnp.stack([sm, ty])
    tc = send("c", sm)
    qay, qbx = at(qay, qbx)
    q00 = rows_cat(qa, qay, qb, qby)
    q10 = send("c", q00)
    qaxy, qbxy = at(qaxy, qbxy)
    q01 = rows_cat(qax, qaxy, qbx, qbxy)
    q11 = send("c", q01)
    oax, oby = send("x", oa), send("y", ob)
    tc = at(tc)
    vecs, bias_up, bias_proj = unpack(jnp.stack([sm, tc]))
    q10, q11, bias_proj, vecs, bias_up = at(q10, q11, bias_proj, vecs, bias_up)
    wq = [[q00, q01], [q10, q11]]
    proj = at(project(at(stream_rel), wq, bias_proj, 3 * lanes))
    oax, oby, far = tie([oax, oby, other(cotangent)], [proj])
    oa, ob = rows_cat(oa, oax), rows_cat(ob, oby)
    oya, oxb = send("y", oa), send("x", ob)
    ctx0 = attend(info, proj, lanes, 0, deps=[oa, ob])
    oya, oxb = tie([oya, oxb], [ctx0])
    wo0 = rows_cat(oa, oya, ob, oxb)
    wo1 = send("c", wo0)
    cot_theirs = send("x", far)
    ctx1 = attend(info, proj, lanes, 1, deps=[wo0])
    tile = own // 2
    block = 2 * lanes
    zhat1, r1, mixed, m_own, ctx_rel = mix(
        ctx0, ctx1, own_seq, wo0, wo1, perm_ctx, vecs, tile, deps=[cot_theirs]
    )
    m_far = send("x", m_own)
    h_own, g_own = up_gelu(m_own, wi, bias_up, block)
    h_far, g_far = up_gelu(m_far, wi, bias_up, block, deps=[h_own])
    p_far = matmul(h_far, wb, 2 * block, BF)
    p_theirs = send("x", p_far)
    p_own = matmul(h_own, wb, 2 * block, F32, deps=[p_far])
    cot = rows_cat(mine(cotangent), cot_theirs)
    live = jnp.broadcast_to(live[:, None], (rows, lanes))
    result, grad_sum2, gb_own, sums2 = turn(p_own, p_theirs, mixed, cot, live, vecs, tile)

    def whole(both, got):
        return jnp.where(x == 0, jnp.stack([both, got]), jnp.stack([got, both]))

    def finish(a, b, n):
        parts = a[n:].astype(BF), b[:n].astype(BF), b[n:].astype(BF)
        got = [lax.ppermute(v, *routes[-1 - i]) for i, v in enumerate(parts)]
        return lambda: add(a[:n], got[0]) + add(got[1], got[2])

    def join(a_near, a_far, b_near, b_far, a, b):
        a1, b1 = add(a_far, a[1]).astype(BF), add(b_far, b[1]).astype(BF)
        got = send("x", a1), send("y", b1)
        return got, add(a_near, a[0]), add(b_near, b[0]), a1

    def half_rows(v):
        e = v.shape[0] // 2
        return v[:e], v[e:]

    def half_cols(v):
        e = v.shape[1] // 2
        return v[:, :e], v[:, e:]

    def join_rows(keep_a, keep_b, a, b):
        return join(*half_rows(keep_a), *half_rows(keep_b), half_rows(a), half_rows(b))

    def join_cols(keep_a, keep_b, a, b):
        return join(*half_cols(keep_a), *half_rows(keep_b), half_cols(a), half_rows(b))

    def joined(got, a, b, _, n):
        got = at(*got)
        return add(a, got[0]), add(b, got[1]), n

    nt = ((1,), (1,))
    gb_far = send("x", gb_own)
    d_own, us0 = down_grad(gb_own, wb, g_own, block)
    d_far, us1 = down_grad(gb_far, wb, g_far, block, deps=[d_own])
    dm_far = dot(d_far, wi, nt).astype(BF)
    dm_theirs = send("x", dm_far)
    back = (dot(h_own, gb_own, TN) + dot(h_far, gb_far, TN)).astype(BF)
    back_done = lax.psum_scatter(back, "dp", scatter_dimension=0, tiled=True)
    dm_own = dot(d_own, wi, nt)
    grad_sum1, grad_att, grad_ctx, sums1 = unmix(
        dm_own, dm_theirs, grad_sum2, zhat1, r1, wo0, wo1, perm_ctx, vecs, own, deps=[back]
    )
    inner = (dot(m_own, d_own, TN) + dot(m_far, d_far, TN)).astype(BF)
    in_done = lax.psum_scatter(inner, "dp", scatter_dimension=0, tiled=True)
    lo_theirs = send("x", result[own:])
    c0, c1 = half_cols(ctx_rel)
    o_core = dot(c1, grad_att, TN).astype(BF)
    o_got = send("c", o_core)
    dp0, ps0 = attend_grad(info, proj, at(grad_ctx), lanes, 0, deps=[inner, o_core])
    dp0, o_got = at(dp0, o_got)
    ok_a, os_a, ok_b, os_b = weight_rows(c0, grad_att, o_got, deps=[dp0])
    oa_got, ob_got = send("y", os_a), send("x", os_b)
    dp1, ps1 = attend_grad(info, proj, at(grad_ctx), lanes, 1, deps=[os_a])
    dp1 = at(dp1)
    s0, s1 = half_cols(stream_rel)
    q_core = jnp.concatenate([dot(s1, r, TN).astype(BF) for r in (dp0, dp1)], axis=1)
    q_got = send("c", q_core)
    o_join = join_rows(ok_a, ok_b, oa_got, ob_got)
    qk_a, qs_a, qk_b, qs_b = weight_cols(s0, dp0, dp1, q_got)
    qa_got, qb_got = send("y", qs_a), send("x", qs_b)
    grad_stream = stream_grad(dp0, dp1, wq, perm_in, grad_sum1, own, deps=[qs_a])
    grad_stream, qa_got, qb_got = at(grad_stream, qa_got, qb_got)
    q_join = join_cols(qk_a, qk_b, qa_got, qb_got)
    out_done = finish(*joined(*o_join, w_out.shape[0]))
    gs_theirs = send("x", grad_stream[own:])
    qkv_done = finish(*joined(*q_join, qs.shape[0]))

    proj_sum = jnp.concatenate([ps0, ps1], axis=1).reshape(2, groups, 3, lanes)
    bias_grad = [proj_sum[:, :, j].reshape(2, dp, bw).transpose(1, 0, 2) for j in (0, 2)]
    up_sum = jnp.stack([us0 + us1, jnp.zeros_like(us0)])

    def widen(v):
        return jnp.pad(v, ((0, 0), (0, 0), (0, lanes - v.shape[2])))

    def both_halves(v):
        return jnp.broadcast_to(widen(v.reshape(dp, 1, dw)), (dp, 2, lanes))

    tiny = [up_sum.reshape(2, dp, lanes).transpose(1, 0, 2)]
    tiny += [both_halves(v) for v in (sums1[0], sums2[0], sums1[1], sums1[2], sums2[1], sums2[2])]
    tiny += [widen(v) for v in bias_grad]
    tiny += [jnp.zeros_like(tiny[0])] * 7
    tiny = jnp.stack(tiny, axis=2)
    tiny = jnp.einsum(
        "nr,nxql->rxql", rel_at.astype(F32), tiny, precision=lax.Precision.HIGHEST
    ).reshape(2, 2, 4, 2, 16, lanes)

    (tiny,) = tie([tiny], [qs_a])
    tiny = tiny[0] + send("c", tiny[1].astype(BF)).astype(F32)
    tiny = tiny[0] + send("y", tiny[1].astype(BF)).astype(F32)
    tiny = tiny[:, 0] + send("x", tiny[:, 1].astype(BF)).astype(F32)
    t = finish(tiny[:2], tiny[2:], 1)()[0]
    layer_out = whole(result[:own], lo_theirs)
    grad_stream = whole(grad_stream[:own], gs_theirs)

    return (
        layer_out,
        grad_stream,
        qkv_done().reshape(-1, groups, 3, lanes).transpose(0, 2, 1, 3).reshape(w_qkv.shape),
        t[7:9, :bw].T,
        out_done(),
        in_done.astype(F32),
        t[0],
        back_done.astype(F32),
        t[1:3, :dw].T,
        t[3:7, :dw].T,
    )


def solution(mesh):
    in_specs = (
        P("dp", "tensor", None),
        P(),
        P("dp"),
        P("dp", "tensor", None),
        P("dp", None, "tensor"),
        P(("tensor", "dp"), None),
        P(("tensor", "dp"), None),
        P("dp", "tensor"),
        P(("tensor", "dp")),
        P(("tensor", "dp"), None),
        P("dp", None),
        P("dp", None),
    )
    out_specs = (
        P("dp", "tensor", None),
        P("dp", "tensor", None),
        P("dp", None, "tensor"),
        P(("tensor", "dp"), None),
        P(("tensor", "dp"), None),
        P("dp", "tensor"),
        P(("tensor", "dp")),
        P(("tensor", "dp"), None),
        P("dp", None),
        P("dp", None),
    )
    here = dict(mesh.shape)
    paired = here["tensor"] == 2 and here["dp"] == 16
    return jax.shard_map(
        one_sequence if paired else per_device, mesh=mesh, in_specs=in_specs, out_specs=out_specs, check_vma=False
    )
```

```python
import functools

import jax
import jax.numpy as jnp
from jax import lax
from jax.experimental import pallas as pl
from jax.experimental.pallas import tpu as pltpu
from jax.sharding import PartitionSpec as P

HD = 64
BF = jnp.bfloat16
F32 = jnp.float32
VMEM = 56 * 1024 * 1024


def norm_rows(summed, gain, offset):
    centred = summed - jnp.mean(summed, axis=-1, keepdims=True)
    variance = jnp.mean(centred * centred, axis=-1, keepdims=True)
    return centred * lax.rsqrt(variance + 1e-06) * gain + offset


def exact_gelu(values):
    return jax.nn.gelu(values, approximate=False)


def per_device(
    stream, lengths, assignment, cotangent, w_qkv, b_qv, w_out, w_in, b_in, w_back, gains, shifts
):
    count = jnp.sum(lengths).astype(jnp.float32)
    all_seqs = lengths.shape[0]
    matches = assignment[:, None] == jnp.arange(all_seqs, dtype=jnp.int32)[None, :]
    slot_len = jnp.sum(jnp.where(matches, lengths[None, :], 0), axis=1)
    (
        projection_weight,
        mixing_weight,
        up_weight,
        down_weight,
        bias_qv,
        bias_up,
        gain_all,
        shift_all,
    ) = (
        lax.all_gather(w_qkv, "dp", axis=0, tiled=True),
        lax.all_gather(w_out, "dp", axis=0, tiled=True),
        lax.all_gather(w_in, "dp", axis=0, tiled=True),
        lax.all_gather(w_back, "dp", axis=0, tiled=True),
        lax.all_gather(b_qv, "dp", axis=0, tiled=True),
        lax.all_gather(b_in, "dp", axis=0, tiled=True),
        lax.all_gather(gains, "dp", axis=0, tiled=True),
        lax.all_gather(shifts, "dp", axis=0, tiled=True),
    )
    seqs_dev, rows_dev, width = stream.shape
    full_rows = rows_dev * lax.axis_size("tensor")
    local_width = projection_weight.shape[2]
    shape_heads = (seqs_dev, full_rows, local_width // HD, HD)
    scale = HD ** (-0.5)
    gain_f = gain_all.astype(jnp.float32)
    shift_f = shift_all.astype(jnp.float32)
    bias_f = bias_qv.astype(jnp.float32)
    gathered_rows = lax.all_gather(stream, "tensor", axis=1, tiled=True)
    projected_rows = jnp.einsum(
        "bpo,orn->bprn", gathered_rows, projection_weight, preferred_element_type=jnp.float32
    )
    queries = (projected_rows[:, :, 0] + bias_f[:, 0]).astype(jnp.bfloat16).reshape(shape_heads)
    key_rows = projected_rows[:, :, 1].astype(jnp.bfloat16).reshape(shape_heads)
    value_rows = (projected_rows[:, :, 2] + bias_f[:, 1]).astype(jnp.bfloat16).reshape(shape_heads)
    allowed = jnp.arange(full_rows, dtype=jnp.int32)[None, :] < slot_len[:, None]
    products = jnp.einsum("sqhe,skhe->shqk", queries, key_rows, preferred_element_type=jnp.float32)
    scores = jnp.where(allowed[:, None, None, :], products * scale, -1e30)
    highest_score = jnp.max(scores, axis=-1, keepdims=True)
    expo = jnp.exp(scores - highest_score)
    weights = expo / jnp.sum(expo, axis=-1, keepdims=True)
    weights_low = weights.astype(jnp.bfloat16)
    context_rows = jnp.einsum(
        "shqk,skhe->sqhe", weights_low, value_rows, preferred_element_type=jnp.float32
    )
    context_rows = context_rows.reshape(seqs_dev, full_rows, local_width).astype(jnp.bfloat16)
    attention_terms = jnp.einsum(
        "kqz,zw->kqw", context_rows, mixing_weight, preferred_element_type=jnp.float32
    )
    attended = (
        lax.psum_scatter(
            attention_terms.astype(jnp.bfloat16), "tensor", scatter_dimension=1, tiled=True
        ).astype(jnp.float32)
        + shift_f[:, 1]
    )
    mixed, first_pull = jax.vjp(
        norm_rows, stream.astype(jnp.float32) + attended, gain_f[:, 0], shift_f[:, 0]
    )
    mixed_every_row = lax.all_gather(mixed.astype(jnp.bfloat16), "tensor", axis=1, tiled=True)
    inner = jnp.einsum(
        "vrw,wy->vry", mixed_every_row, up_weight, preferred_element_type=jnp.float32
    ) + bias_up.astype(jnp.float32)
    hidden, gelu_pull = jax.vjp(exact_gelu, inner)
    hidden_reduced = hidden.astype(jnp.bfloat16)
    perceptron_terms = jnp.einsum(
        "kqz,zw->kqw", hidden_reduced, down_weight, preferred_element_type=jnp.float32
    )
    branch = (
        lax.psum_scatter(
            perceptron_terms.astype(jnp.bfloat16), "tensor", scatter_dimension=1, tiled=True
        ).astype(jnp.float32)
        + shift_f[:, 3]
    )
    result, second_pull = jax.vjp(norm_rows, mixed + branch, gain_f[:, 1], shift_f[:, 2])
    position = lax.axis_index("tensor") * rows_dev + jnp.arange(rows_dev, dtype=jnp.int32)
    live = (position[None, :] < slot_len[:, None]).astype(jnp.float32)
    factor = jnp.float32(seqs_dev * lax.axis_size("dp") * full_rows) / count
    seed_grad = cotangent.astype(jnp.float32) * live[:, :, None] * factor
    grad_sum2, grad_gain2, grad_shift2 = second_pull(seed_grad)
    grad_branch = grad_sum2.astype(jnp.bfloat16)
    branch_bias_grad = jnp.sum(grad_branch.astype(jnp.float32), axis=(0, 1))
    branch_every_row = lax.all_gather(grad_branch, "tensor", axis=1, tiled=True)
    down_part = jnp.einsum(
        "irk,irt->kt", hidden_reduced, branch_every_row, preferred_element_type=jnp.float32
    )
    hidden_gradient = jnp.einsum(
        "atj,gj->atg", branch_every_row, down_weight, preferred_element_type=jnp.float32
    )
    inner_gradient = gelu_pull(hidden_gradient)[0].astype(jnp.bfloat16)
    up_bias_part = jnp.sum(inner_gradient.astype(jnp.float32), axis=(0, 1))
    up_portion = jnp.einsum(
        "pna,pnb->ab", mixed_every_row, inner_gradient, preferred_element_type=jnp.float32
    )
    mixed_partial_terms = jnp.einsum(
        "yjc,oc->yjo", inner_gradient, up_weight, preferred_element_type=jnp.float32
    )
    grad_mixed = grad_sum2 + lax.psum_scatter(
        mixed_partial_terms.astype(jnp.bfloat16), "tensor", scatter_dimension=1, tiled=True
    ).astype(jnp.float32)
    grad_sum1, grad_gain1, grad_shift1 = first_pull(grad_mixed)
    grad_attended = grad_sum1.astype(jnp.bfloat16)
    mix_bias_grad = jnp.sum(grad_attended.astype(jnp.float32), axis=(0, 1))
    attended_every_row = lax.all_gather(grad_attended, "tensor", axis=1, tiled=True)
    mixing_portion = jnp.einsum(
        "irk,irt->kt", context_rows, attended_every_row, preferred_element_type=jnp.float32
    )
    grad_context = jnp.einsum(
        "atj,gj->atg", attended_every_row, mixing_weight, preferred_element_type=jnp.float32
    )
    grad_context = grad_context.astype(jnp.bfloat16).reshape(shape_heads)
    grad_values = jnp.einsum(
        "shqk,sqhe->skhe", weights_low, grad_context, preferred_element_type=jnp.float32
    ).astype(jnp.bfloat16)
    grad_weights = jnp.einsum(
        "sqhe,skhe->shqk", grad_context, value_rows, preferred_element_type=jnp.float32
    )
    grad_scores = weights * (grad_weights - jnp.sum(weights * grad_weights, axis=-1, keepdims=True))
    grad_products = (grad_scores * scale).astype(jnp.bfloat16)
    grad_queries = jnp.einsum(
        "shqk,skhe->sqhe", grad_products, key_rows, preferred_element_type=jnp.float32
    ).astype(jnp.bfloat16)
    grad_keys = jnp.einsum(
        "shqk,sqhe->skhe", grad_products, queries, preferred_element_type=jnp.float32
    ).astype(jnp.bfloat16)
    flat_shape = (seqs_dev, full_rows, local_width)
    projection_gradient = jnp.stack(
        [
            grad_queries.reshape(flat_shape),
            grad_keys.reshape(flat_shape),
            grad_values.reshape(flat_shape),
        ],
        axis=2,
    )
    proj_bias_part = jnp.stack(
        [
            jnp.sum(grad_queries.astype(jnp.float32).reshape(flat_shape), axis=(0, 1)),
            jnp.sum(grad_values.astype(jnp.float32).reshape(flat_shape), axis=(0, 1)),
        ],
        axis=1,
    )
    projection_portion = jnp.einsum(
        "tqj,tquk->juk", gathered_rows, projection_gradient, preferred_element_type=jnp.float32
    )
    stream_terms = jnp.einsum(
        "wvjo,xjo->wvx", projection_gradient, projection_weight, preferred_element_type=jnp.float32
    )
    grad_stream = grad_sum1 + lax.psum_scatter(
        stream_terms.astype(jnp.bfloat16), "tensor", scatter_dimension=1, tiled=True
    ).astype(jnp.float32)
    gain_part = jnp.stack([grad_gain1, grad_gain2], axis=1)
    shift_part = jnp.stack([grad_shift1, mix_bias_grad, grad_shift2, branch_bias_grad], axis=1)
    proj_done, proj_bias_done, mix_done, up_done, up_bias_done, down_done, gain_done, shift_done = (
        lax.psum_scatter(
            projection_portion.astype(jnp.bfloat16), "dp", scatter_dimension=0, tiled=True
        ).astype(jnp.float32),
        lax.psum_scatter(
            proj_bias_part.astype(jnp.bfloat16), "dp", scatter_dimension=0, tiled=True
        ).astype(jnp.float32),
        lax.psum_scatter(
            mixing_portion.astype(jnp.bfloat16), "dp", scatter_dimension=0, tiled=True
        ).astype(jnp.float32),
        lax.psum_scatter(
            up_portion.astype(jnp.bfloat16), "dp", scatter_dimension=0, tiled=True
        ).astype(jnp.float32),
        lax.psum_scatter(
            up_bias_part.astype(jnp.bfloat16), "dp", scatter_dimension=0, tiled=True
        ).astype(jnp.float32),
        lax.psum_scatter(
            down_part.astype(jnp.bfloat16), "dp", scatter_dimension=0, tiled=True
        ).astype(jnp.float32),
        lax.psum_scatter(
            gain_part.astype(jnp.bfloat16), "dp", scatter_dimension=0, tiled=True
        ).astype(jnp.float32),
        lax.psum_scatter(
            shift_part.astype(jnp.bfloat16), "dp", scatter_dimension=0, tiled=True
        ).astype(jnp.float32),
    )
    gain_total, shift_total = lax.psum((gain_done, shift_done), "tensor")
    return (
        result.astype(jnp.bfloat16),
        grad_stream.astype(jnp.bfloat16),
        proj_done,
        proj_bias_done,
        mix_done,
        up_done,
        up_bias_done,
        down_done,
        gain_total,
        shift_total,
    )


def kernel(body, name, grid, in_specs, out_specs, out_shape, args, *, scratch=(), prefetch=0, deps=()):
    inputs = prefetch + len(in_specs)

    def without_deps(*refs):
        body(*refs[:inputs], *refs[inputs + len(deps) :])

    return pl.pallas_call(
        without_deps,
        grid_spec=pltpu.PrefetchScalarGridSpec(
            num_scalar_prefetch=prefetch,
            grid=grid,
            in_specs=list(in_specs) + [pl.BlockSpec(memory_space=pl.ANY)] * len(deps),
            out_specs=out_specs,
            scratch_shapes=scratch,
        ),
        out_shape=out_shape,
        compiler_params=pltpu.CompilerParams(vmem_limit_bytes=VMEM),
        name=name,
    )(*args, *deps)


def gelu_terms(v):
    density = jnp.exp(v * v * -0.5)
    t = 1.0 / (1.0 + (0.3275911 * 0.7071067811865476) * jnp.abs(v))
    poly = t * (
        0.254829592
        + t * (-0.284496736 + t * (1.421413741 + t * (-1.453152027 + t * 1.061405429)))
    )
    tail = 0.5 * poly * density
    return jnp.where(v >= 0, 1.0 - tail, tail), density * 0.3989422804014327


def dot(a, b, dims=((1,), (0,))):
    return lax.dot_general(a, b, (dims, ((), ())), preferred_element_type=F32)


def project_body(a_ref, w00, w10, w01, w11, b_ref, o_ref, *, half):
    j = pl.program_id(0)
    k = w00.shape[0]

    def go(w0, w1):
        acc = dot(a_ref[:, :k], w0[...]) + dot(a_ref[:, k:], w1[...]) + b_ref[...]
        o_ref[...] = acc.astype(o_ref.dtype)

    @pl.when(j < half)
    def _():
        go(w00, w10)

    @pl.when(j >= half)
    def _():
        go(w01, w11)


def split_specs(rows, block, half):
    low = pl.BlockSpec((rows, block), lambda j, *_: (0, jnp.minimum(j, half - 1)))
    high = pl.BlockSpec((rows, block), lambda j, *_: (0, jnp.maximum(j - half, 0)))
    return [low, low, high, high]


def project(a, w, bias, block, deps=()):
    rows, width = a.shape
    cols = w[0][0].shape[1]
    half = cols // block
    return kernel(
        functools.partial(project_body, half=half),
        "project",
        (2 * half,),
        [pl.BlockSpec((rows, width), lambda j: (0, 0))]
        + split_specs(width // 2, block, half)
        + [pl.BlockSpec((1, block), lambda j: (0, j))],
        pl.BlockSpec((rows, block), lambda j: (0, j)),
        jax.ShapeDtypeStruct((rows, 2 * cols), BF),
        (a, w[0][0], w[1][0], w[0][1], w[1][1], bias,),
        deps=deps,
    )


def up_body(a_ref, w_ref, b_ref, h_ref, g_ref, acc):
    new = dot(a_ref[...], w_ref[...])
    v = acc[...]
    cdf, density = gelu_terms(v)
    h_ref[...] = (v * cdf).astype(BF)
    g_ref[...] = (cdf + v * density).astype(BF)
    acc[...] = new + b_ref[...]


def up_gelu(a, w, bias, block, deps=()):
    rows, width = a.shape
    cols = w.shape[1]
    end = cols // block - 1
    out = jax.ShapeDtypeStruct((rows, cols), BF)
    spot = pl.BlockSpec((rows, block), lambda j: (0, jnp.maximum(j - 1, 0)))
    return kernel(
        up_body,
        "up_gelu",
        (end + 2,),
        [
            whole_of(a),
            pl.BlockSpec((width, block), lambda j: (0, jnp.minimum(j, end))),
            pl.BlockSpec((1, block), lambda j: (0, jnp.minimum(j, end))),
        ],
        [spot, spot],
        [out, out],
        (a, w, bias),
        scratch=[pltpu.VMEM((rows, block), F32)],
        deps=deps,
    )


def matmul_body(a_ref, w_ref, o_ref):
    o_ref[...] = dot(a_ref[...], w_ref[...]).astype(o_ref.dtype)


def matmul(a, w, block, dtype, deps=()):
    return kernel(
        matmul_body,
        "matmul",
        (w.shape[1] // block,),
        [whole_of(a), pl.BlockSpec((w.shape[0], block), lambda j: (0, j))],
        pl.BlockSpec((a.shape[0], block), lambda j: (0, j)),
        jax.ShapeDtypeStruct((a.shape[0], w.shape[1]), dtype),
        (a, w),
        deps=deps,
    )


def down_grad_body(a_ref, w_ref, g_ref, d_ref, s_ref):
    d = dot(a_ref[...], w_ref[...], ((1,), (1,)))
    d = (d * g_ref[...].astype(F32)).astype(BF)
    d_ref[...] = d
    s_ref[...] = jnp.sum(d.astype(F32), axis=0, keepdims=True)


def down_grad(a, w, g, block, deps=()):
    rows, width = a.shape
    cols = g.shape[1]
    return kernel(
        down_grad_body,
        "down_grad",
        (cols // block,),
        [
            whole_of(a),
            pl.BlockSpec((block, width), lambda j: (j, 0)),
            pl.BlockSpec((rows, block), lambda j: (0, j)),
        ],
        [
            pl.BlockSpec((rows, block), lambda j: (0, j)),
            pl.BlockSpec((1, block), lambda j: (0, j)),
        ],
        [jax.ShapeDtypeStruct((rows, cols), BF), jax.ShapeDtypeStruct((1, cols), F32)],
        (a, w, g),
        deps=deps,
    )


def head_weights(info, q, k, rows):
    own = rows // 2
    at = lax.broadcasted_iota(jnp.int32, (1, rows), 1)
    first = info[1] * own
    pos = jnp.where(at < own, at + first, at - first)
    s = dot(q, k, ((1,), (1,)))
    s = jnp.where(pos < info[0], s * HD ** (-0.5), -1e30)
    e = jnp.exp(s - jnp.max(s, axis=1, keepdims=True))
    return e * (1.0 / jnp.sum(e, axis=1, keepdims=True))


def attend_body(info, p_ref, c_ref):
    rows, lanes = c_ref.shape
    for h in range(lanes // HD):
        part = [p_ref[:, j * lanes + h * HD : j * lanes + (h + 1) * HD] for j in range(3)]
        w = head_weights(info, part[0], part[1], rows).astype(BF)
        c_ref[:, h * HD : (h + 1) * HD] = dot(w, part[2]).astype(BF)


def attend_grad_body(info, p_ref, t_ref, d_ref, s_ref):
    rows, lanes = t_ref.shape
    tn = ((0,), (0,))
    for h in range(lanes // HD):
        q, k, v = [p_ref[:, j * lanes + h * HD : j * lanes + (h + 1) * HD] for j in range(3)]
        t = t_ref[:, h * HD : (h + 1) * HD]
        w = head_weights(info, q, k, rows)
        dw = dot(t, v, ((1,), (1,)))
        ds = w * (dw - jnp.sum(w * dw, axis=1, keepdims=True)) * HD ** (-0.5)
        ds = ds.astype(BF)
        outs = (dot(ds, k), dot(ds, q, tn), dot(w.astype(BF), t, tn))
        for j in range(3):
            at = slice(j * lanes + h * HD, j * lanes + (h + 1) * HD)
            low = outs[j].astype(BF)
            d_ref[:, at] = low
            s_ref[:, at] = jnp.sum(low.astype(F32), axis=0, keepdims=True)


def attend(info, proj, lanes, part, deps=()):
    rows, cols = proj.shape
    steps = cols // (6 * lanes)
    return kernel(
        attend_body,
        "attend",
        (steps,),
        [pl.BlockSpec((rows, 3 * lanes), lambda j, info: (0, j + part * steps))],
        pl.BlockSpec((rows, lanes), lambda j, info: (0, j)),
        jax.ShapeDtypeStruct((rows, cols // 6), BF),
        (info, proj,),
        prefetch=1,
        deps=deps,
    )


def attend_grad(info, proj, top, lanes, part, deps=()):
    rows, cols = proj.shape
    steps = cols // (6 * lanes)
    return kernel(
        attend_grad_body,
        "attend_grad",
        (steps,),
        [
                pl.BlockSpec((rows, 3 * lanes), lambda j, info: (0, j + part * steps)),
                pl.BlockSpec((rows, lanes), lambda j, info: (0, j + part * steps)),
            ],
        [
                pl.BlockSpec((rows, 3 * lanes), lambda j, info: (0, j)),
                pl.BlockSpec((1, 3 * lanes), lambda j, info: (0, j)),
            ],
        [
            jax.ShapeDtypeStruct((rows, cols // 2), BF),
            jax.ShapeDtypeStruct((1, cols // 2), F32),
        ],
        (info, proj, top,),
        prefetch=1,
        deps=deps,
    )


def whole_of(v):
    return pl.BlockSpec(v.shape, lambda *_: (0,) * v.ndim)


def tile_of(v, tile):
    return pl.BlockSpec((tile, v.shape[1]), lambda j: (j, 0))


def norm_of(z):
    centred = z - jnp.mean(z, axis=1, keepdims=True)
    r = lax.rsqrt(jnp.mean(centred * centred, axis=1, keepdims=True) + 1e-06)
    return centred * r, r


def norm_grad(t, zhat, r, gain):
    gt = t * gain
    mean = jnp.mean(gt, axis=1, keepdims=True)
    return r * (gt - mean - zhat * jnp.mean(gt * zhat, axis=1, keepdims=True))


def gather_sums(s_ref, *values):
    sums = [jnp.sum(v, axis=0, keepdims=True) for v in values]
    sums += [jnp.zeros_like(sums[0])] * (8 - len(sums))
    sums = jnp.concatenate(sums, axis=0)

    @pl.when(pl.program_id(0) == 0)
    def _():
        s_ref[...] = sums

    @pl.when(pl.program_id(0) != 0)
    def _():
        s_ref[...] += sums


def mix_body(c0, c1, s_ref, w0, w1, pc, v_ref, zh_ref, r_ref, m_ref, mr_ref, x_ref):
    h = w0.shape[0]
    ctx = dot(c0[...], pc[:h, :]) + dot(c1[...], pc[h:, :])
    ctx = ctx.astype(BF)
    x_ref[...] = ctx
    att = dot(ctx[:, :h], w0[...]) + dot(ctx[:, h:], w1[...]) + v_ref[3:4, :]
    zhat, r = norm_of(s_ref[...].astype(F32) + att)
    zh_ref[...] = zhat
    r_ref[...] = jnp.broadcast_to(r, r_ref.shape)
    mixed = zhat * v_ref[0:1, :] + v_ref[2:3, :]
    m_ref[...] = mixed
    mr_ref[...] = mixed.astype(BF)


def mix(c0, c1, stream, w0, w1, perm_ctx, vecs, tile, deps=()):
    rows, width = stream.shape
    full = jax.ShapeDtypeStruct((rows, width), F32)
    low = jax.ShapeDtypeStruct((rows, width), BF)
    outs = [full, jax.ShapeDtypeStruct((rows, 128), F32), full, low, low]
    return kernel(
        mix_body,
        "mix",
        (rows // tile,),
        [tile_of(v, tile) for v in (c0, c1, stream)]
        + [whole_of(v) for v in (w0, w1, perm_ctx, vecs)],
        [tile_of(v, tile) for v in outs],
        outs,
        (c0, c1, stream, w0, w1, perm_ctx, vecs,),
        deps=deps,
    )


def turn_body(p_ref, t_ref, m_ref, c_ref, l_ref, v_ref, o_ref, g_ref, gb_ref, s_ref):
    branch = p_ref[...] + t_ref[...].astype(F32) + v_ref[5:6, :]
    zhat, r = norm_of(m_ref[...] + branch)
    gain = v_ref[1:2, :]
    o_ref[...] = (zhat * gain + v_ref[4:5, :]).astype(BF)
    seed = c_ref[...].astype(F32) * l_ref[:, 0:1]
    g = norm_grad(seed, zhat, r, gain)
    g_ref[...] = g
    low = g.astype(BF)
    gb_ref[...] = low
    gather_sums(s_ref, seed * zhat, seed, low.astype(F32))


def turn(part, theirs, mixed, cot, live, vecs, tile, deps=()):
    rows, width = mixed.shape
    full = jax.ShapeDtypeStruct((rows, width), F32)
    low = jax.ShapeDtypeStruct((rows, width), BF)
    sums = jax.ShapeDtypeStruct((8, width), F32)
    tiled = (part, theirs, mixed, cot, live)
    return kernel(
        turn_body,
        "turn",
        (rows // tile,),
        [tile_of(v, tile) for v in tiled] + [whole_of(vecs)],
        [tile_of(v, tile) for v in (low, full, low)] + [whole_of(sums)],
        [low, full, low, sums],
        (*tiled, vecs),
        deps=deps,
    )


def unmix_body(p_ref, t_ref, g2, zh, r_ref, wo0, wo1, pc, v_ref, g1_ref, ga_ref, gc_ref, s_ref):
    nt = ((1,), (1,))
    grad = g2[...] + p_ref[...] + t_ref[...].astype(F32)
    zhat = zh[...]
    g1 = norm_grad(grad, zhat, r_ref[:, 0:1], v_ref[0:1, :])
    g1_ref[...] = g1
    low = g1.astype(BF)
    ga_ref[...] = low
    ctx = jnp.concatenate([dot(low, wo0[...], nt), dot(low, wo1[...], nt)], axis=1)
    gc_ref[...] = dot(ctx.astype(BF), pc[...], nt).astype(BF)
    gather_sums(s_ref, grad * zhat, grad, low.astype(F32))


def unmix(part, theirs, g2, zhat, r, wo0, wo1, perm_ctx, vecs, tile, deps=()):
    rows, width = g2.shape
    full = jax.ShapeDtypeStruct((rows, width), F32)
    low = jax.ShapeDtypeStruct((rows, width), BF)
    sums = jax.ShapeDtypeStruct((8, width), F32)
    tiled = (part, theirs, g2, zhat, r)
    fixed = (wo0, wo1, perm_ctx, vecs)
    return kernel(
        unmix_body,
        "unmix",
        (rows // tile,),
        [tile_of(v, tile) for v in tiled] + [whole_of(v) for v in fixed],
        [tile_of(v, tile) for v in (full, low, low)] + [whole_of(sums)],
        [full, low, low, sums],
        tiled + fixed,
        deps=deps,
    )


def stream_body(d0, d1, w00, w10, w01, w11, pi, g1, o_ref):
    nt = ((1,), (1,))
    parts = [
        dot(d0[...], u[...], nt) + dot(d1[...], v[...], nt) for u, v in ((w00, w01), (w10, w11))
    ]
    back = jnp.concatenate(parts, axis=1).astype(BF)
    o_ref[...] = (g1[...] + dot(back, pi[...], nt)).astype(BF)


def stream_grad(d0, d1, w, perm_in, g1, tile, deps=()):
    out = jax.ShapeDtypeStruct(g1.shape, BF)
    ws = (w[0][0], w[1][0], w[0][1], w[1][1])
    return kernel(
        stream_body,
        "stream_grad",
        (g1.shape[0] // tile,),
        [tile_of(d0, tile), tile_of(d1, tile)]
        + [whole_of(v) for v in ws + (perm_in,)]
        + [tile_of(g1, tile)],
        tile_of(out, tile),
        out,
        (d0, d1, *ws, perm_in, g1,),
        deps=deps,
    )


TN = ((0,), (0,))


def rows_body(l_ref, r_ref, *refs, added, per):
    grad = dot(l_ref[...], r_ref[...], TN)
    if not added:
        refs[0][...] = grad.astype(BF)
        return
    grad = (grad + refs[0][...].astype(F32)).astype(BF)
    j = pl.program_id(0)
    for i in range(4):

        @pl.when(j // per == i)
        def _():
            refs[1 + i][...] = grad


def weight_rows(left, right, got=None, deps=()):
    tokens, k = left.shape
    n = right.shape[1]
    per = 2 if k // 8 % 128 == 0 else 1
    block = k // (4 * per)
    row = pl.BlockSpec((block, n), lambda j: (j, 0))
    outs, out_specs, more = [jax.ShapeDtypeStruct((k, n), BF)], [row], []
    if got is not None:
        outs = [jax.ShapeDtypeStruct((k // 4, n), BF)] * 4
        out_specs = [
            pl.BlockSpec((block, n), lambda j, i=i: (jnp.clip(j - per * i, 0, per - 1), 0))
            for i in range(4)
        ]
        more = [got]
    return kernel(
        functools.partial(rows_body, added=got is not None, per=per),
        "weight_rows",
        (4 * per,),
        [pl.BlockSpec((tokens, block), lambda j: (0, j)), whole_of(right)]
        + [row] * len(more),
        out_specs,
        outs,
        (left, right, *more,),
        deps=deps,
    )


def cols_body(l_ref, r0, r1, *refs, half, added):
    j = pl.program_id(0)
    turned = refs[-1]

    @pl.when(j == 0)
    def _():
        turned[...] = l_ref[...].T

    def go(r, high):
        grad = dot(turned[...], r[...])
        if not added:
            refs[0][...] = grad.astype(BF)
            return
        got, keep_a, send_a, keep_b, send_b = refs[:5]
        q = grad.shape[0] // 4
        grad = (grad + got[...].astype(F32)).astype(BF)
        keep_a[...] = grad[:q]
        send_a[...] = grad[q : 2 * q]
        if high:
            send_b[...] = grad[2 * q :]
        else:
            keep_b[...] = grad[2 * q :]

    @pl.when(j < half)
    def _():
        go(r0, False)

    @pl.when(j >= half)
    def _():
        go(r1, True)


def weight_cols(left, r0, r1, got=None, deps=()):
    tokens, k = left.shape
    n = r0.shape[1]
    block = 512
    half = n // block
    low = pl.BlockSpec((tokens, block), lambda j: (0, jnp.minimum(j, half - 1)))
    high = pl.BlockSpec((tokens, block), lambda j: (0, jnp.maximum(j - half, 0)))
    full = pl.BlockSpec((k, block), lambda j: (0, j))
    outs, out_specs, more = [jax.ShapeDtypeStruct((k, 2 * n), BF)], [full], []
    if got is not None:
        a = jax.ShapeDtypeStruct((k // 4, 2 * n), BF)
        b = jax.ShapeDtypeStruct((k // 2, n), BF)
        outs = [a, a, b, b]
        sa = pl.BlockSpec((k // 4, block), lambda j: (0, j))
        out_specs = [
            sa,
            sa,
            pl.BlockSpec((k // 2, block), lambda j: (0, jnp.minimum(j, half - 1))),
            pl.BlockSpec((k // 2, block), lambda j: (0, jnp.maximum(j - half, 0))),
        ]
        more = [got]
    return kernel(
        functools.partial(cols_body, half=half, added=got is not None),
        "weight_cols",
        (2 * half,),
        [whole_of(left), low, high] + [full] * len(more),
        out_specs,
        outs,
        (left, r0, r1, *more,),
        scratch=[pltpu.VMEM((k, tokens), BF)],
        deps=deps,
    )


def tie_body(*refs):
    pass


def tie(values, deps=()):
    spot = pl.BlockSpec(memory_space=pl.ANY)
    return pl.pallas_call(
        tie_body,
        in_specs=[spot] * (len(values) + len(deps)),
        out_specs=[spot] * len(values),
        out_shape=[jax.ShapeDtypeStruct(v.shape, v.dtype) for v in values],
        input_output_aliases={i: i for i in range(len(values))},
        name="tie",
    )(*values, *deps)


class Order:
    def __init__(self):
        self.token = jnp.zeros((8, 128), F32)

    def at(self, *values):
        values, self.token = lax.optimization_barrier((values, self.token))
        return values if len(values) > 1 else values[0]


def rows_cat(*parts):
    return jnp.concatenate(parts, axis=0)


def one_sequence(
    stream, lengths, assignment, cotangent, w_qkv, b_qv, w_out, w_in, b_in, w_back, gains, shifts
):
    _, own, width = stream.shape
    rows = 2 * own
    dp = lax.axis_size("dp")
    x = lax.axis_index("tensor")
    spot = lax.axis_index("dp")
    zi, yi, ci = spot // 4, (spot // 2) % 2, spot % 2
    lanes = 128

    order = Order()
    at = order.at
    routes = {
        "x": ("tensor", [(0, 1), (1, 0)]),
        "y": ("dp", [(i, i ^ 2) for i in range(dp)]),
        "c": ("dp", [(i, i ^ 1) for i in range(dp)]),
    }
    for k in range(1, 4):
        routes[k] = ("dp", [(i, (i + 4 * k) % dp) for i in range(dp)])
        routes[-k] = ("dp", [(i, (i - 4 * k) % dp) for i in range(dp)])

    def send(way, value):
        return lax.ppermute(at(value), *routes[way])

    def along_z(value):
        value = at(value)
        return [lax.ppermute(value, *routes[k]) for k in range(1, 4)]

    def other(v):
        return lax.dynamic_index_in_dim(v, 1 - x, 0, keepdims=False)

    def mine(v):
        return lax.dynamic_index_in_dim(v, x, 0, keepdims=False)

    n = jnp.arange(dp, dtype=jnp.int32)
    slot = (zi - n // 4) % 4
    first_half = slot < 2
    y_rel = (n // 2) % 2 ^ yi
    c_rel = n % 2 ^ ci
    k2 = slot % 2
    col_place = (slot // 2) * 4 + y_rel * 2 + k2

    def row_place(x_rel):
        return jnp.where(first_half, y_rel * 4 + x_rel * 2 + k2, 8 + x_rel * 4 + y_rel * 2 + k2)

    def one_hot(dest, size):
        return (dest[:, None] == jnp.arange(size, dtype=jnp.int32)[None, :]).astype(BF)

    def spread(block_dest, block):
        count = block_dest.shape[0]
        dest = block_dest[:, None] * block + jnp.arange(block, dtype=jnp.int32)[None, :]
        return one_hot(dest.reshape(-1), count * block)

    perm_in = spread(c_rel * (dp // 2) + col_place, width // dp)
    perm_ctx = spread(
        jnp.concatenate([c_rel * dp + row_place(0), c_rel * dp + row_place(1)]), width // (2 * dp)
    )
    place = x[None].astype(jnp.int32)

    def lane_rows(v):
        v = v.astype(BF)
        return jnp.pad(v, ((0, 0), (0, lanes - v.shape[1])))

    small = jnp.concatenate(
        [
            b_in.reshape(1, lanes),
            lane_rows(gains.T),
            lane_rows(shifts.T),
            lane_rows(b_qv.T),
            jnp.zeros((7, lanes), BF),
        ],
        axis=0,
    )

    def add(u, v):
        return u.astype(F32) + v.astype(F32)

    groups = width // 2 // lanes
    hw = width // 2
    qs = w_qkv.reshape(-1, 3, groups, lanes).transpose(0, 2, 1, 3).reshape(-1, 3 * hw)

    count = jnp.sum(lengths).astype(F32)
    all_seqs = lengths.shape[0]
    matches = mine(assignment) == jnp.arange(all_seqs, dtype=jnp.int32)
    slot_len = jnp.sum(jnp.where(matches, lengths, 0))
    info = jnp.stack([slot_len, x]).astype(jnp.int32)
    row = jnp.arange(rows, dtype=jnp.int32)
    position = jnp.where(row < own, row + x * own, row - x * own)
    factor = F32(all_seqs * rows) / count
    live = jnp.where(position < slot_len, factor, 0.0)
    info, live, perm_in, perm_ctx, place, rel_at = (
        info,
        live,
        perm_in,
        perm_ctx,
        place,
        one_hot(c_rel * 8 + y_rel * 4 + slot, dp),
    )

    dw = width // dp
    bw = width // (2 * dp)

    def unpack(sm):
        sm = sm.transpose(0, 1, 3, 2, 4, 5).reshape(dp, 2, 16, lanes)
        sm = jnp.einsum("nr,rxql->nxql", rel_at, sm, preferred_element_type=F32)
        vecs = sm[:, 0, 1:9, :dw].transpose(1, 0, 2).reshape(8, width)
        bias_up = sm[:, 0, 0].reshape(1, -1)
        bias = sm[:, :, 7:9, :bw].transpose(2, 1, 0, 3).reshape(2, 2, groups, 1, lanes)
        bias = jnp.concatenate([bias[0], jnp.zeros_like(bias[0]), bias[1]], axis=2)
        return vecs, bias_up, bias.reshape(1, -1)

    q1, q2, q3 = along_z(qs)
    theirs = send("x", other(stream))
    t1, t2, t3 = along_z(small)
    q1, q2, q3, perm_in, perm_ctx = tie([q1, q2, q3, perm_in, perm_ctx], [theirs, t1, t2, t3])
    qa, qb = rows_cat(qs, q1), rows_cat(q2, q3)
    qax, qby = send("x", qa), send("y", qb)
    o1, o2, o3 = along_z(w_out)
    sm = jnp.stack([small, t1, t2, t3])
    tx = send("x", sm)
    theirs = at(theirs)
    own_seq = rows_cat(mine(stream), theirs)
    stream_rel = dot(own_seq, perm_in).astype(BF)
    in_shard, back_shard = tie([w_in, w_back], [q1, q2, q3])
    wi = lax.all_gather(in_shard, "dp", axis=0, tiled=True)
    wb = lax.all_gather(back_shard, "dp", axis=0, tiled=True)
    qax, qby = at(qax, qby)
    qay, qaxy, qbx, qbxy = send("y", qa), send("y", qax), send("x", qb), send("x", qby)
    tx = at(tx)
    sm = jnp.stack([sm, tx])
    ty = send("y", sm)
    o1, o2, o3 = at(o1, o2, o3)
    oa, ob = rows_cat(w_out, o1), rows_cat(o2, o3)
    ty = at(ty)
    sm = jnp.stack([sm, ty])
    tc = send("c", sm)
    qay, qbx = at(qay, qbx)
    q00 = rows_cat(qa, qay, qb, qby)
    q10 = send("c", q00)
    qaxy, qbxy = at(qaxy, qbxy)
    q01 = rows_cat(qax, qaxy, qbx, qbxy)
    q11 = send("c", q01)
    oax, oby = send("x", oa), send("y", ob)
    tc = at(tc)
    vecs, bias_up, bias_proj = unpack(jnp.stack([sm, tc]))
    q10, q11, bias_proj, vecs, bias_up = at(q10, q11, bias_proj, vecs, bias_up)
    wq = [[q00, q01], [q10, q11]]
    proj = at(project(at(stream_rel), wq, bias_proj, 3 * lanes))
    oax, oby, far = tie([oax, oby, other(cotangent)], [proj])
    oa, ob = rows_cat(oa, oax), rows_cat(ob, oby)
    oya, oxb = send("y", oa), send("x", ob)
    ctx0 = attend(info, proj, lanes, 0, deps=[oa, ob])
    oya, oxb = tie([oya, oxb], [ctx0])
    wo0 = rows_cat(oa, oya, ob, oxb)
    wo1 = send("c", wo0)
    cot_theirs = send("x", far)
    ctx1 = attend(info, proj, lanes, 1, deps=[wo0])
    tile = own // 2
    block = 2 * lanes
    zhat1, r1, mixed, m_own, ctx_rel = mix(
        ctx0, ctx1, own_seq, wo0, wo1, perm_ctx, vecs, own, deps=[cot_theirs]
    )
    m_far = send("x", m_own)
    h_own, g_own = up_gelu(m_own, wi, bias_up, block)
    h_far, g_far = up_gelu(m_far, wi, bias_up, block, deps=[h_own])
    p_far = matmul(h_far, wb, 2 * block, BF)
    p_theirs = send("x", p_far)
    p_own = matmul(h_own, wb, 2 * block, F32, deps=[p_far])
    cot = rows_cat(mine(cotangent), cot_theirs)
    live = jnp.broadcast_to(live[:, None], (rows, lanes))
    result, grad_sum2, gb_own, sums2 = turn(p_own, p_theirs, mixed, cot, live, vecs, tile)

    def whole(both, got):
        return jnp.where(x == 0, jnp.stack([both, got]), jnp.stack([got, both]))

    def finish(a, b, n):
        parts = a[n:].astype(BF), b[:n].astype(BF), b[n:].astype(BF)
        got = [lax.ppermute(v, *routes[-1 - i]) for i, v in enumerate(parts)]
        return lambda: add(a[:n], got[0]) + add(got[1], got[2])

    def join(a_near, a_far, b_near, b_far, a, b):
        a1, b1 = add(a_far, a[1]).astype(BF), add(b_far, b[1]).astype(BF)
        got = send("x", a1), send("y", b1)
        return got, add(a_near, a[0]), add(b_near, b[0]), a1

    def half_rows(v):
        e = v.shape[0] // 2
        return v[:e], v[e:]

    def half_cols(v):
        e = v.shape[1] // 2
        return v[:, :e], v[:, e:]

    def join_rows(keep_a, keep_b, a, b):
        return join(*half_rows(keep_a), *half_rows(keep_b), half_rows(a), half_rows(b))

    def join_cols(keep_a, keep_b, a, b):
        return join(*half_cols(keep_a), *half_rows(keep_b), half_cols(a), half_rows(b))

    def joined(got, a, b, _, n):
        got = at(*got)
        return add(a, got[0]), add(b, got[1]), n

    nt = ((1,), (1,))
    gb_far = send("x", gb_own)
    d_own, us0 = down_grad(gb_own, wb, g_own, block)
    d_far, us1 = down_grad(gb_far, wb, g_far, block, deps=[d_own])
    dm_far = dot(d_far, wi, nt).astype(BF)
    dm_theirs = send("x", dm_far)
    back = (dot(h_own, gb_own, TN) + dot(h_far, gb_far, TN)).astype(BF)
    back_done = lax.psum_scatter(back, "dp", scatter_dimension=0, tiled=True)
    dm_own = dot(d_own, wi, nt)
    grad_sum1, grad_att, grad_ctx, sums1 = unmix(
        dm_own, dm_theirs, grad_sum2, zhat1, r1, wo0, wo1, perm_ctx, vecs, own, deps=[back]
    )
    inner = (dot(m_own, d_own, TN) + dot(m_far, d_far, TN)).astype(BF)
    in_done = lax.psum_scatter(inner, "dp", scatter_dimension=0, tiled=True)
    lo_theirs = send("x", result[own:])
    c0, c1 = half_cols(ctx_rel)
    o_core = dot(c1, grad_att, TN).astype(BF)
    o_got = send("c", o_core)
    dp0, ps0 = attend_grad(info, proj, at(grad_ctx), lanes, 0, deps=[inner, o_core])
    dp0, o_got = at(dp0, o_got)
    ok_a, os_a, ok_b, os_b = weight_rows(c0, grad_att, o_got, deps=[dp0])
    oa_got, ob_got = send("y", os_a), send("x", os_b)
    dp1, ps1 = attend_grad(info, proj, at(grad_ctx), lanes, 1, deps=[os_a])
    dp1 = at(dp1)
    s0, s1 = half_cols(stream_rel)
    q_core = jnp.concatenate([dot(s1, r, TN).astype(BF) for r in (dp0, dp1)], axis=1)
    q_got = send("c", q_core)
    o_join = join_rows(ok_a, ok_b, oa_got, ob_got)
    qk_a, qs_a, qk_b, qs_b = weight_cols(s0, dp0, dp1, q_got)
    qa_got, qb_got = send("y", qs_a), send("x", qs_b)
    grad_stream = stream_grad(dp0, dp1, wq, perm_in, grad_sum1, own, deps=[qs_a])
    grad_stream, qa_got, qb_got = at(grad_stream, qa_got, qb_got)
    q_join = join_cols(qk_a, qk_b, qa_got, qb_got)
    out_done = finish(*joined(*o_join, w_out.shape[0]))
    gs_theirs = send("x", grad_stream[own:])
    qkv_done = finish(*joined(*q_join, qs.shape[0]))

    proj_sum = jnp.concatenate([ps0, ps1], axis=1).reshape(2, groups, 3, lanes)
    bias_grad = [proj_sum[:, :, j].reshape(2, dp, bw).transpose(1, 0, 2) for j in (0, 2)]
    up_sum = jnp.stack([us0 + us1, jnp.zeros_like(us0)])

    def widen(v):
        return jnp.pad(v, ((0, 0), (0, 0), (0, lanes - v.shape[2])))

    def both_halves(v):
        return jnp.broadcast_to(widen(v.reshape(dp, 1, dw)), (dp, 2, lanes))

    tiny = [up_sum.reshape(2, dp, lanes).transpose(1, 0, 2)]
    tiny += [both_halves(v) for v in (sums1[0], sums2[0], sums1[1], sums1[2], sums2[1], sums2[2])]
    tiny += [widen(v) for v in bias_grad]
    tiny += [jnp.zeros_like(tiny[0])] * 7
    tiny = jnp.stack(tiny, axis=2)
    tiny = jnp.einsum(
        "nr,nxql->rxql", rel_at.astype(F32), tiny, precision=lax.Precision.HIGHEST
    ).reshape(2, 2, 4, 2, 16, lanes)

    (tiny,) = tie([tiny], [qs_a])
    tiny = tiny[0] + send("c", tiny[1].astype(BF)).astype(F32)
    tiny = tiny[0] + send("y", tiny[1].astype(BF)).astype(F32)
    tiny = tiny[:, 0] + send("x", tiny[:, 1].astype(BF)).astype(F32)
    t = finish(tiny[:2], tiny[2:], 1)()[0]
    layer_out = whole(result[:own], lo_theirs)
    grad_stream = whole(grad_stream[:own], gs_theirs)

    return (
        layer_out,
        grad_stream,
        qkv_done().reshape(-1, groups, 3, lanes).transpose(0, 2, 1, 3).reshape(w_qkv.shape),
        t[7:9, :bw].T,
        out_done(),
        in_done.astype(F32),
        t[0],
        back_done.astype(F32),
        t[1:3, :dw].T,
        t[3:7, :dw].T,
    )


def solution(mesh):
    in_specs = (
        P("dp", "tensor", None),
        P(),
        P("dp"),
        P("dp", "tensor", None),
        P("dp", None, "tensor"),
        P(("tensor", "dp"), None),
        P(("tensor", "dp"), None),
        P("dp", "tensor"),
        P(("tensor", "dp")),
        P(("tensor", "dp"), None),
        P("dp", None),
        P("dp", None),
    )
    out_specs = (
        P("dp", "tensor", None),
        P("dp", "tensor", None),
        P("dp", None, "tensor"),
        P(("tensor", "dp"), None),
        P(("tensor", "dp"), None),
        P("dp", "tensor"),
        P(("tensor", "dp")),
        P(("tensor", "dp"), None),
        P("dp", None),
        P("dp", None),
    )
    here = dict(mesh.shape)
    paired = here["tensor"] == 2 and here["dp"] == 16
    return jax.shard_map(
        one_sequence if paired else per_device, mesh=mesh, in_specs=in_specs, out_specs=out_specs, check_vma=False
    )
```
